128 devices in a mesh: dp: 2 (over z_lo), tm: 4 (over z_hi, core), height: 16 (over y, x).
Axes of the slice: x: 4, y: 4, z: 4 (z_hi: 2, z_lo: 2; z = z_hi * 2 + z_lo), core: 2. Of those that a mesh axis runs over, the one named last changes fastest.
Arguments:
- clip: bfloat16 [2, 12, 64, 128, 128], P('dp', 'tm', 'height'), may hold values from -6 to 6
- first_weight: bfloat16 [3, 3, 3, 128, 128], replicated, may hold values from -0.109375 to 0.109375
- second_weight: bfloat16 [3, 3, 3, 128, 128], replicated, may hold values from -0.109375 to 0.109375
- cotangent: bfloat16 [2, 12, 64, 128, 128], P('dp', 'tm', 'height'), may hold values from -6 to 6
Outputs:
- output: bfloat16 [2, 12, 64, 128, 128], P('dp', 'tm', 'height')
- clip_grad: bfloat16 [2, 12, 64, 128, 128], P('dp', 'tm', 'height')
- first_grad: float32 [3, 3, 3, 128, 128], replicated
- second_grad: float32 [3, 3, 3, 128, 128], replicated
The draws below stay inside these ranges and needn't reach their ends.
All inputs are finite; a program needn't handle non-finite values.
Results may differ from the reference program's by a relative error of at most 0.0085.
Values may be sent and summed in bfloat16 or wider, within the bound.
No kernel may reach another device: no remote copies, remote signals or barrier semaphores. Data moves between devices by JAX's collectives and lax.ppermute only.
A program may use at most 128 MiB of HBM per device.

```python
import math
import jax
import jax.numpy as jnp
from jax import lax

C = 128
W = 128
B = 2
FRAMES = 12
ROWS = 64


def shard_levels(key, shape, cuts, smallest, high):
    gain = 1.0
    for position, shards_of in cuts:
        heights = jax.random.uniform(jax.random.fold_in(jax.random.fold_in(key, 6), position), (shards_of,), jnp.float32, smallest / len(cuts), high / len(cuts))
        gain = gain * jnp.repeat(jnp.exp(heights), shape[position] // shards_of).reshape((-1,) + (1,) * (len(shape) - 1 - position))
    return gain


def noise(own_key, dims, deviation, bound, shards=(), held_as=jnp.bfloat16):
    entries = deviation * jax.random.normal(own_key, dims, jnp.float32)
    if shards:
        entries = entries * shard_levels(own_key, dims, shards, -0.22, 0.18)
    return jnp.clip(entries, -bound, bound).astype(held_as)


def setup_inputs(seed: int = 0) -> dict:
    key_of = jax.random.split(jax.random.key(seed), 5)
    clip = noise(key_of[0], (B, FRAMES, ROWS, W, C), 1.0, 6.0, ((0, 2), (1, 4), (2, 16)))
    first_weight = noise(key_of[1], (3, 3, 3, C, C), (27 * C) ** -0.5, 0.109375)
    second_weight = noise(key_of[2], (3, 3, 3, C, C), (27 * C) ** -0.5, 0.109375)
    cotangent = noise(key_of[3], (B, FRAMES, ROWS, W, C), 1.0, 6.0, ((0, 2), (1, 4), (2, 16)))
    return {"clip": clip, "first_weight": first_weight, "second_weight": second_weight, "cotangent": cotangent}


def causal_conv(field, kernel):
    return lax.conv_general_dilated(field, kernel, (1, 1, 1), [(2, 0), (1, 1), (1, 1)], dimension_numbers=('NDHWC', 'DHWIO', 'NDHWC'), precision=lax.Precision.HIGHEST)

def slope(value):
    sigmoid_value = jax.nn.sigmoid(value)
    return sigmoid_value * (1.0 + value * (1.0 - sigmoid_value))

def widen(array):
    return array.astype(jnp.float32)

def reference(clip, first_weight, second_weight, cotangent):
    pre_one = causal_conv(widen(clip), widen(first_weight))
    hidden = jax.nn.silu(pre_one).astype(jnp.bfloat16)
    pre_two = causal_conv(widen(hidden), widen(second_weight))
    output = jax.nn.silu(pre_two).astype(jnp.bfloat16)
    grad_two = (widen(cotangent) * slope(pre_two)).astype(jnp.bfloat16)
    _, back_two = jax.vjp(causal_conv, widen(hidden), widen(second_weight))
    grad_hidden, second_raw = back_two(widen(grad_two))
    grad_one = (grad_hidden * slope(pre_one)).astype(jnp.bfloat16)
    _, back_one = jax.vjp(causal_conv, widen(clip), widen(first_weight))
    clip_wide, first_raw = back_one(widen(grad_one))
    scale = 1.0 / math.sqrt(B * FRAMES * ROWS * W)
    return (output, clip_wide.astype(jnp.bfloat16), first_raw * scale, second_raw * scale)
```

```python
import functools
import math

import jax
import jax.numpy as jnp
from jax import lax
from jax.experimental import pallas as pl
from jax.experimental.pallas import tpu as pltpu
from jax.sharding import PartitionSpec as P

ALL = ("dp", "tm", "height")
PARAMS = pltpu.CompilerParams(vmem_limit_bytes=48 * 1024 * 1024)
VMEM = pl.BlockSpec(memory_space=pltpu.VMEM)
TAPS = [(a, b) for a in range(3) for b in range(3)]


def call(kernel, outs, scratch, flops, *args):
    moved = sum(x.size * x.dtype.itemsize for x in (*args, *outs))
    return pl.pallas_call(
        kernel,
        out_shape=outs,
        in_specs=[VMEM] * len(args),
        out_specs=[VMEM] * len(outs),
        scratch_shapes=scratch,
        compiler_params=PARAMS,
        cost_estimate=pl.CostEstimate(flops=flops, bytes_accessed=moved, transcendentals=0),
    )(*args)


def lay(pad, centre, time, low, high, ahead):
    frames, rows = centre.shape[:2]
    first = 0 if ahead else 2
    pad[first : first + frames, 1 : 1 + rows] = centre[...]
    first = frames if ahead else 0
    pad[first : first + 2, 1 : 1 + rows] = time[...]
    pad[:, 0:1] = low[...]
    pad[:, 1 + rows :] = high[...]


def down(value, columns):
    row = lax.broadcasted_iota(jnp.int32, value.shape, 0) % columns
    return jnp.where(row == 0, 0.0, pltpu.roll(value, 1, 0))


def up(value, columns):
    row = lax.broadcasted_iota(jnp.int32, value.shape, 0) % columns
    return jnp.where(row == columns - 1, 0.0, pltpu.roll(value, value.shape[0] - 1, 0))


def convolve(pad, taps, frame, rows, transposed):
    columns, channels = pad.shape[2:]
    parts = []
    for a, b in TAPS:
        t, h = (frame + 2 - a, 2 - b) if transposed else (frame + a, b)
        parts.append(pad[t, h : h + rows].reshape(rows * columns, channels))
    stacked = jnp.concatenate(parts, axis=1)
    dims = (((1,), (1 if transposed else 0,)), ((), ()))
    product = lax.dot_general(stacked, taps[...], dims, preferred_element_type=jnp.float32)
    left, middle, right = (product[:, c * channels : (c + 1) * channels] for c in range(3))
    if transposed:
        left, right = right, left
    return down(left, columns) + middle + up(right, columns)


def lay_taps(taps, kernel, transposed):
    c_in, c_out = kernel.shape[3:]
    for place, (a, b) in enumerate(TAPS):
        for c in range(3):
            if transposed:
                taps[c * c_in : (c + 1) * c_in, place * c_out : (place + 1) * c_out] = kernel[a, b, c]
            else:
                taps[place * c_in : (place + 1) * c_in, c * c_out : (c + 1) * c_out] = kernel[a, b, c]


def first_kernel(centre, time, low, high, kernel, slope, hidden, pad, taps):
    lay(pad, centre, time, low, high, False)
    lay_taps(taps, kernel, False)
    frames, rows = centre.shape[:2]
    for t in range(frames):
        z = convolve(pad, taps, t, rows, False)
        s = jax.nn.sigmoid(z)
        slope[t] = (s * (1.0 + z * (1.0 - s))).reshape(slope.shape[1:])
        hidden[t] = (z * s).astype(jnp.bfloat16).reshape(hidden.shape[1:])


def second_kernel(centre, time, low, high, kernel, cotangent, output, grad, pad, taps):
    lay(pad, centre, time, low, high, False)
    lay_taps(taps, kernel, False)
    frames, rows = centre.shape[:2]
    for t in range(frames):
        z = convolve(pad, taps, t, rows, False)
        s = jax.nn.sigmoid(z)
        output[t] = (z * s).astype(jnp.bfloat16).reshape(output.shape[1:])
        steep = (s * (1.0 + z * (1.0 - s))).reshape(grad.shape[1:])
        grad[t] = (cotangent[t].astype(jnp.float32) * steep).astype(jnp.bfloat16)


def back_kernel(centre, time, low, high, kernel, *rest):
    slope, (grad, pad, taps) = rest[:-3], rest[-3:]
    lay(pad, centre, time, low, high, True)
    lay_taps(taps, kernel, True)
    frames, rows = centre.shape[:2]
    for t in range(frames):
        z = convolve(pad, taps, t, rows, True).reshape(grad.shape[1:])
        if slope:
            z = z * slope[0][t]
        grad[t] = z.astype(jnp.bfloat16)


def weight_kernel(centre, time, low, high, grad, out, pad, moved):
    lay(pad, centre, time, low, high, False)
    frames, rows, columns, channels = centre.shape
    cells = frames * rows * columns
    wide = grad[...].reshape(cells, channels).astype(jnp.float32)
    moved[:, :channels] = up(wide, columns).astype(jnp.bfloat16)
    moved[:, channels : 2 * channels] = grad[...].reshape(cells, channels)
    moved[:, 2 * channels :] = down(wide, columns).astype(jnp.bfloat16)
    dims = (((0,), (0,)), ((), ()))
    for a, b in TAPS:
        block = pad[a : a + frames, b : b + rows].reshape(cells, channels)
        product = lax.dot_general(block, moved[...], dims, preferred_element_type=jnp.float32)
        for c in range(3):
            out[a, b, c] = product[:, c * channels : (c + 1) * channels].astype(out.dtype)


def edges(block, ahead):
    count, line = lax.axis_size("tm"), lax.axis_size("height")
    step = -1 if ahead else 1
    route = [(i, i + step) for i in range(count) if 0 <= i + step < count]
    time = lax.ppermute(block[:2] if ahead else block[-2:], "tm", route)
    whole = jnp.concatenate([block, time] if ahead else [time, block], axis=0)
    forward = [(i, i + 1) for i in range(line - 1)]
    backward = [(j, i) for i, j in forward]
    low = lax.ppermute(whole[:, -1:], "height", forward)
    high = lax.ppermute(whole[:, :1], "height", backward)
    return time, low, high


def body(clip, first_weight, second_weight, cotangent):
    _, frames, rows, columns, channels = clip.shape
    cells = frames * rows * columns
    clip, cotangent = clip[0], cotangent[0]
    flops = 2 * cells * 27 * channels * channels
    shape = (frames, rows, columns, channels)
    bf16 = jax.ShapeDtypeStruct(shape, jnp.bfloat16)
    f32 = jax.ShapeDtypeStruct(shape, jnp.float32)
    raw = jax.ShapeDtypeStruct((3, 3, 3, channels, channels), jnp.bfloat16)
    pad = pltpu.VMEM((frames + 2, rows + 2, columns, channels), jnp.bfloat16)
    taps = pltpu.VMEM((9 * channels, 3 * channels), jnp.bfloat16)
    back_taps = pltpu.VMEM((3 * channels, 9 * channels), jnp.bfloat16)
    moved = pltpu.VMEM((cells, 3 * channels), jnp.bfloat16)

    clip_edges = edges(clip, False)
    slope, hidden = call(first_kernel, [f32, bf16], [pad, taps], flops, clip, *clip_edges, first_weight)
    hidden_edges = edges(hidden, False)
    output, grad_two = call(
        second_kernel, [bf16, bf16], [pad, taps], flops, hidden, *hidden_edges, second_weight, cotangent
    )
    two_edges = edges(grad_two, True)
    (second_raw,) = call(weight_kernel, [raw], [pad, moved], flops, hidden, *hidden_edges, grad_two)
    (grad_one,) = call(back_kernel, [bf16], [pad, back_taps], flops, grad_two, *two_edges, second_weight, slope)
    one_edges = edges(grad_one, True)
    (first_raw,) = call(weight_kernel, [raw], [pad, moved], flops, clip, *clip_edges, grad_one)
    (clip_grad,) = call(back_kernel, [bf16], [pad, back_taps], flops, grad_one, *one_edges, first_weight)

    devices = lax.axis_size(ALL)
    scale = 1.0 / math.sqrt(cells * devices)
    both = jnp.stack([first_raw, second_raw]).reshape(devices, -1, channels)
    terms = lax.all_to_all(both, ALL, 0, 0, tiled=True)
    total = jnp.sum(terms.astype(jnp.float32), axis=0).astype(jnp.bfloat16)
    spread = jnp.broadcast_to(total[None], both.shape)
    sums = lax.all_to_all(spread, ALL, 0, 0, tiled=True).reshape(2, *raw.shape)
    sums = sums.astype(jnp.float32) * scale
    return output[None], clip_grad[None], sums[0], sums[1]


def solution(mesh):
    block = P("dp", "tm", "height", None, None)
    return jax.shard_map(
        body,
        mesh=mesh,
        in_specs=(block, P(), P(), block),
        out_specs=(block, block, P(), P()),
        check_vma=False,
    )
```

```python
import functools
import math

import jax
import jax.numpy as jnp
from jax import lax
from jax.experimental import pallas as pl
from jax.experimental.pallas import tpu as pltpu
from jax.sharding import PartitionSpec as P

ALL = ("dp", "tm", "height")
PARAMS = pltpu.CompilerParams(vmem_limit_bytes=48 * 1024 * 1024)
VMEM = pl.BlockSpec(memory_space=pltpu.VMEM)
TAPS = [(a, b) for a in range(3) for b in range(3)]


def call(kernel, outs, scratch, flops, *args):
    moved = sum(x.size * x.dtype.itemsize for x in (*args, *outs))
    return pl.pallas_call(
        kernel,
        out_shape=outs,
        in_specs=[VMEM] * len(args),
        out_specs=[VMEM] * len(outs),
        scratch_shapes=scratch,
        compiler_params=PARAMS,
        cost_estimate=pl.CostEstimate(flops=flops, bytes_accessed=moved, transcendentals=0),
    )(*args)


def lay(pad, centre, time, near, far, corners, ahead):
    frames, rows = centre.shape[:2]
    place, above = near_row(rows + 2), far_row(rows + 2)
    own = pl.ds(0 if ahead else 2, frames)
    beyond = pl.ds(frames if ahead else 0, 2)
    pad[own, 1 : 1 + rows] = centre[...]
    pad[own, pl.ds(place, 1)] = near[...]
    pad[own, pl.ds(above, 1)] = far[...]
    pad[beyond, 1 : 1 + rows] = time[...]
    pad[beyond, pl.ds(place, 1)] = corners[:, 0:1]
    pad[beyond, pl.ds(above, 1)] = corners[:, 1:2]

    def clear(at):
        pad[at] = jnp.zeros_like(pad[at])

    line, tm = lax.axis_index("height"), lax.axis_index("tm")
    pl.when(line == 0)(lambda: clear((slice(None), slice(0, 1))))
    pl.when(line == lax.axis_size("height") - 1)(lambda: clear((slice(None), slice(rows + 1, rows + 2))))
    pl.when(tm == (lax.axis_size("tm") - 1 if ahead else 0))(lambda: clear((beyond,)))


def near_row(rows):
    return (1 - lax.axis_index("height") % 2) * (rows - 1)


def far_row(rows):
    return lax.axis_index("height") % 2 * (rows - 1)


def strips(block, last, near, far, ahead):
    frames, rows = block.shape[:2]
    last[...] = block[0:2] if ahead else block[frames - 2 :]
    near[...] = block[:, pl.ds(near_row(rows), 1)]
    far[...] = block[:, pl.ds(far_row(rows), 1)]


def down(value, columns):
    row = lax.broadcasted_iota(jnp.int32, value.shape, 0) % columns
    return jnp.where(row == 0, 0.0, pltpu.roll(value, 1, 0))


def up(value, columns):
    row = lax.broadcasted_iota(jnp.int32, value.shape, 0) % columns
    return jnp.where(row == columns - 1, 0.0, pltpu.roll(value, value.shape[0] - 1, 0))


def convolve(pad, taps, frame, rows, transposed):
    columns, channels = pad.shape[2:]
    parts = []
    for a, b in TAPS:
        t, h = (frame + 2 - a, 2 - b) if transposed else (frame + a, b)
        parts.append(pad[t, h : h + rows].reshape(rows * columns, channels))
    stacked = jnp.concatenate(parts, axis=1)
    dims = (((1,), (1 if transposed else 0,)), ((), ()))
    product = lax.dot_general(stacked, taps[...], dims, preferred_element_type=jnp.float32)
    left, middle, right = (product[:, c * channels : (c + 1) * channels] for c in range(3))
    if transposed:
        left, right = right, left
    return down(left, columns) + middle + up(right, columns)


def lay_taps(taps, kernel, transposed):
    c_in, c_out = kernel.shape[3:]
    for place, (a, b) in enumerate(TAPS):
        for c in range(3):
            if transposed:
                taps[c * c_in : (c + 1) * c_in, place * c_out : (place + 1) * c_out] = kernel[a, b, c]
            else:
                taps[place * c_in : (place + 1) * c_in, c * c_out : (c + 1) * c_out] = kernel[a, b, c]


def first_kernel(centre, time, near, far, corners, kernel, slope, hidden, last, near_out, far_out, pad, taps):
    lay(pad, centre, time, near, far, corners, False)
    lay_taps(taps, kernel, False)
    frames, rows = centre.shape[:2]
    for t in range(frames):
        z = convolve(pad, taps, t, rows, False)
        s = jax.nn.sigmoid(z)
        slope[t] = (s * (1.0 + z * (1.0 - s))).reshape(slope.shape[1:])
        hidden[t] = (z * s).astype(jnp.bfloat16).reshape(hidden.shape[1:])
    strips(hidden, last, near_out, far_out, False)


def second_kernel(
    centre, time, near, far, corners, kernel, cotangent, output, grad, last, near_out, far_out, pad, taps
):
    lay(pad, centre, time, near, far, corners, False)
    lay_taps(taps, kernel, False)
    frames, rows = centre.shape[:2]
    for t in range(frames):
        z = convolve(pad, taps, t, rows, False)
        s = jax.nn.sigmoid(z)
        output[t] = (z * s).astype(jnp.bfloat16).reshape(output.shape[1:])
        steep = (s * (1.0 + z * (1.0 - s))).reshape(grad.shape[1:])
        grad[t] = (cotangent[t].astype(jnp.float32) * steep).astype(jnp.bfloat16)
    strips(grad, last, near_out, far_out, True)


def back_kernel(centre, time, near, far, corners, kernel, grad, pad, taps):
    lay(pad, centre, time, near, far, corners, True)
    lay_taps(taps, kernel, True)
    frames, rows = centre.shape[:2]
    for t in range(frames):
        z = convolve(pad, taps, t, rows, True)
        grad[t] = z.astype(jnp.bfloat16).reshape(grad.shape[1:])


def back_slope_kernel(
    centre, time, near, far, corners, kernel, slope, grad, last, near_out, far_out, pad, taps
):
    lay(pad, centre, time, near, far, corners, True)
    lay_taps(taps, kernel, True)
    frames, rows = centre.shape[:2]
    for t in range(frames):
        z = convolve(pad, taps, t, rows, True).reshape(grad.shape[1:])
        grad[t] = (z * slope[t]).astype(jnp.bfloat16)
    strips(grad, last, near_out, far_out, True)


def weight_kernel(centre, time, near, far, corners, grad, keep, send, pad, moved):
    lay(pad, centre, time, near, far, corners, False)
    frames, rows, columns, channels = centre.shape
    cells = frames * rows * columns
    core = lax.axis_index("tm") % 2
    wide = grad[...].reshape(cells, channels).astype(jnp.float32)
    moved[:, :channels] = up(wide, columns).astype(jnp.bfloat16)
    moved[:, channels : 2 * channels] = grad[...].reshape(cells, channels)
    moved[:, 2 * channels :] = down(wide, columns).astype(jnp.bfloat16)
    dims = (((0,), (0,)), ((), ()))
    half = channels // 2
    for place, (a, b) in enumerate(TAPS):
        block = pad[a : a + frames, b : b + rows].reshape(cells, channels)
        product = lax.dot_general(block, moved[...], dims, preferred_element_type=jnp.float32)
        for c in range(3):
            part = product[:, c * channels : (c + 1) * channels]
            mine = jnp.where(core == 0, part[:half], part[half:])
            other = jnp.where(core == 0, part[half:], part[:half])
            keep[:, 3 * place + c] = mine.reshape(4, -1, channels)
            send[:, 3 * place + c] = other.astype(jnp.bfloat16).reshape(4, -1, channels)
    for out in (keep, send):
        out[:, 27:] = jnp.zeros_like(out[:, 27:])


def first_scatter_kernel(keep_one, came_one, keep_two, came_two, mine, *sent):
    x = lax.axis_index("height") % 4
    for d, out in enumerate((mine, *sent)):
        for first, keep, came in ((0, keep_one, came_one), (2, keep_two, came_two)):
            total = keep[x ^ d] + came[x ^ d].astype(jnp.float32)
            out[first : first + 2] = total.reshape(2, -1, *total.shape[1:]).astype(out.dtype)


def second_scatter_kernel(own, one, two, three, mine, *sent):
    y = lax.axis_index("height") // 4
    for d, out in enumerate((mine, *sent)):
        own_part, *parts = (ref[y ^ d].astype(jnp.float32) for ref in (own, one, two, three))
        out[...] = ((own_part + parts[0]) + (parts[1] + parts[2])).astype(out.dtype)


def add_kernel(own, one, two, three, out):
    own, one, two, three = (ref[...].astype(jnp.float32) for ref in (own, one, two, three))
    out[...] = ((own + one) + (two + three)).astype(out.dtype)


def join_kernel(own, one, two, three, out):
    y = lax.axis_index("height") // 4
    for d, part in enumerate((own, one, two, three)):
        out[y ^ d] = part[...]


def gather_kernel(scale, *refs):
    outs = refs[-2:]
    x, core = lax.axis_index("height") % 4, lax.axis_index("tm") % 2
    taps = outs[0].shape[0]
    for d in range(4):
        for half in range(2):
            for k, out in enumerate(outs):
                block = refs[4 * half + d][2 * k : 2 * k + 2].astype(jnp.float32) * scale
                block = block.reshape(-1, *block.shape[2:])[:taps]
                out[:, pl.ds((core ^ half) * 4 + (x ^ d), 1)] = block[:, None]


def swap(value, mask):
    return lax.ppermute(value, ALL, [(i, i ^ mask) for i in range(lax.axis_size(ALL))])


def summed(one, two, scale):
    _, taps, part, channels = one[0].shape
    quarter = (taps // 2, part, channels)
    size = 8 * taps * part * channels

    def shapes(shape):
        return [jax.ShapeDtypeStruct(shape, jnp.float32)] + 3 * [jax.ShapeDtypeStruct(shape, jnp.bfloat16)]

    mine, *sent = call(first_scatter_kernel, shapes((4, *quarter)), [], size, *one, *two)
    terms = [mine] + [swap(value, d) for d, value in enumerate(sent, 1)]
    mine, *sent = call(second_scatter_kernel, shapes(quarter), [], size, *terms)
    terms = [mine] + [swap(value, 4 * d) for d, value in enumerate(sent, 1)]
    small = jax.ShapeDtypeStruct(quarter, jnp.bfloat16)
    (total,) = call(add_kernel, [small], [], size // 4, *terms)
    terms = [total] + [swap(total, mask) for mask in (64, 32, 96)]
    (total,) = call(add_kernel, [small], [], size // 4, *terms)
    terms = [total] + [swap(total, 4 * d) for d in (1, 2, 3)]
    (total,) = call(join_kernel, [jax.ShapeDtypeStruct((4, *quarter), jnp.bfloat16)], [], size, *terms)
    parts = [total] + [swap(total, d) for d in (1, 2, 3)]
    parts += [swap(value, 16) for value in parts]
    whole = jax.ShapeDtypeStruct((27, 8, part, channels), jnp.float32)
    outs = call(functools.partial(gather_kernel, scale), [whole, whole], [], 8 * size, *parts)
    return [out.reshape(3, 3, 3, channels, channels) for out in outs]


def edges(last, near, far, ahead):
    count, line = lax.axis_size("tm"), lax.axis_size("height")
    step = -1 if ahead else 1
    route = [(i, (i + step) % count) for i in range(count)]
    time = lax.ppermute(last, "tm", route)
    near = lax.ppermute(near, "height", [(i, i ^ 1) for i in range(line)])
    far = lax.ppermute(far, "height", [(i, (i - 1 if i % 2 == 0 else i + 1) % line) for i in range(line)])
    rows = jnp.concatenate([near, far], axis=1)
    corners = lax.ppermute(rows[:2] if ahead else rows[-2:], "tm", route)
    return time, near, far, corners


def body(clip, first_weight, second_weight, cotangent):
    _, frames, rows, columns, channels = clip.shape
    cells = frames * rows * columns
    clip, cotangent = clip[0], cotangent[0]
    flops = 2 * cells * 27 * channels * channels
    shape = (frames, rows, columns, channels)
    bf16 = jax.ShapeDtypeStruct(shape, jnp.bfloat16)
    f32 = jax.ShapeDtypeStruct(shape, jnp.float32)
    last = jax.ShapeDtypeStruct((2, *shape[1:]), jnp.bfloat16)
    line = jax.ShapeDtypeStruct((frames, 1, *shape[2:]), jnp.bfloat16)
    quarters = (4, 28, channels // 8, channels)
    keep = jax.ShapeDtypeStruct(quarters, jnp.float32)
    send = jax.ShapeDtypeStruct(quarters, jnp.bfloat16)
    pad = pltpu.VMEM((frames + 2, rows + 2, columns, channels), jnp.bfloat16)
    taps = pltpu.VMEM((9 * channels, 3 * channels), jnp.bfloat16)
    back_taps = pltpu.VMEM((3 * channels, 9 * channels), jnp.bfloat16)
    moved = pltpu.VMEM((cells, 3 * channels), jnp.bfloat16)
    scale = 1.0 / math.sqrt(cells * lax.axis_size(ALL))

    even = lax.axis_index("height") % 2 == 0
    top, bottom = clip[:, :1], clip[:, -1:]
    clip_edges = edges(clip[-2:], jnp.where(even, bottom, top), jnp.where(even, top, bottom), False)
    slope, hidden, *cut = call(
        first_kernel, [f32, bf16, last, line, line], [pad, taps], flops, clip, *clip_edges, first_weight
    )
    hidden_edges = edges(*cut, False)
    output, grad_two, *cut = call(
        second_kernel,
        [bf16, bf16, last, line, line],
        [pad, taps],
        flops,
        hidden,
        *hidden_edges,
        second_weight,
        cotangent,
    )
    two_edges = edges(*cut, True)
    mine, other = call(weight_kernel, [keep, send], [pad, moved], flops, hidden, *hidden_edges, grad_two)
    second_terms = (mine, swap(other, 16))
    grad_one, *cut = call(
        back_slope_kernel,
        [bf16, last, line, line],
        [pad, back_taps],
        flops,
        grad_two,
        *two_edges,
        second_weight,
        slope,
    )
    one_edges = edges(*cut, True)
    mine, other = call(weight_kernel, [keep, send], [pad, moved], flops, clip, *clip_edges, grad_one)
    first_grad, second_grad = summed((mine, swap(other, 16)), second_terms, scale)
    (clip_grad,) = call(back_kernel, [bf16], [pad, back_taps], flops, grad_one, *one_edges, first_weight)
    return output[None], clip_grad[None], first_grad, second_grad


def solution(mesh):
    block = P("dp", "tm", "height", None, None)
    return jax.shard_map(
        body,
        mesh=mesh,
        in_specs=(block, P(), P(), block),
        out_specs=(block, block, P(), P()),
        check_vma=False,
    )
```

```python
import functools
import math

import jax
import jax.numpy as jnp
from jax import lax
from jax.experimental import pallas as pl
from jax.experimental.pallas import tpu as pltpu
from jax.sharding import PartitionSpec as P

ALL = ("dp", "tm", "height")
PARAMS = pltpu.CompilerParams(vmem_limit_bytes=48 * 1024 * 1024)
VMEM = pl.BlockSpec(memory_space=pltpu.VMEM)
HBM = pl.BlockSpec(memory_space=pltpu.HBM)
ANY = pl.BlockSpec(memory_space=pl.ANY)
TAPS = [(a, b) for a in range(3) for b in range(3)]


def call(kernel, outs, scratch, flops, *args, after=(), inside=VMEM, outside=()):
    moved = sum(x.size * x.dtype.itemsize for x in (*args, *outs))

    def run(*refs):
        kernel(*refs[: len(args)], *refs[len(args) + len(after) :])

    return pl.pallas_call(
        run,
        out_shape=outs,
        in_specs=[inside] * len(args) + [ANY] * len(after),
        out_specs=list(outside) + [VMEM] * (len(outs) - len(outside)),
        scratch_shapes=scratch,
        compiler_params=PARAMS,
        cost_estimate=pl.CostEstimate(flops=flops, bytes_accessed=moved, transcendentals=0),
    )(*args, *after)


def copied(pairs, sems):
    copies = [pltpu.make_async_copy(source, target, sems.at[i]) for i, (source, target) in enumerate(pairs)]
    for copy in copies:
        copy.start()
    return copies


def cut_kernel(block, whole, last, near, far, sems):
    frames, rows = block.shape[:2]
    pairs = [
        (block.at[:, pl.ds(near_row(rows), 1)], near),
        (block.at[:, pl.ds(far_row(rows), 1)], far),
        (block.at[pl.ds(frames - 2, 2)], last),
        (block, whole),
    ]
    for copy in copied(pairs, sems):
        copy.wait()


def taps_kernel(kernel, taps, held, sems):
    (copy,) = copied([(kernel, held)], sems)
    copy.wait()
    lay_taps(taps, held, False)


def lay(pad, centre, time, near, far, corners, ahead):
    frames, rows = centre.shape[:2]
    place, above = near_row(rows + 2), far_row(rows + 2)
    own = pl.ds(0 if ahead else 2, frames)
    beyond = pl.ds(frames if ahead else 0, 2)
    pad[own, 1 : 1 + rows] = centre[...]
    pad[own, pl.ds(place, 1)] = near[...]
    pad[own, pl.ds(above, 1)] = far[...]
    pad[beyond, 1 : 1 + rows] = time[...]
    pad[beyond, pl.ds(place, 1)] = corners[:, 0:1]
    pad[beyond, pl.ds(above, 1)] = corners[:, 1:2]

    def clear(at):
        pad[at] = jnp.zeros_like(pad[at])

    line, tm = lax.axis_index("height"), lax.axis_index("tm")
    pl.when(line == 0)(lambda: clear((slice(None), slice(0, 1))))
    pl.when(line == lax.axis_size("height") - 1)(lambda: clear((slice(None), slice(rows + 1, rows + 2))))
    pl.when(tm == (lax.axis_size("tm") - 1 if ahead else 0))(lambda: clear((beyond,)))


def near_row(rows):
    return (1 - lax.axis_index("height") % 2) * (rows - 1)


def far_row(rows):
    return lax.axis_index("height") % 2 * (rows - 1)


def strips(block, last, near, far, ahead):
    frames, rows = block.shape[:2]
    last[...] = block[0:2] if ahead else block[frames - 2 :]
    near[...] = block[:, pl.ds(near_row(rows), 1)]
    far[...] = block[:, pl.ds(far_row(rows), 1)]


def down(value, columns):
    row = lax.broadcasted_iota(jnp.int32, value.shape, 0) % columns
    return jnp.where(row == 0, 0.0, pltpu.roll(value, 1, 0))


def up(value, columns):
    row = lax.broadcasted_iota(jnp.int32, value.shape, 0) % columns
    return jnp.where(row == columns - 1, 0.0, pltpu.roll(value, value.shape[0] - 1, 0))


def convolve(pad, taps, frame, rows, transposed):
    columns, channels = pad.shape[2:]
    parts = []
    for a, b in TAPS:
        t, h = (frame + 2 - a, 2 - b) if transposed else (frame + a, b)
        parts.append(pad[t, h : h + rows].reshape(rows * columns, channels))
    stacked = jnp.concatenate(parts, axis=1)
    dims = (((1,), (1 if transposed else 0,)), ((), ()))
    product = lax.dot_general(stacked, taps[...], dims, preferred_element_type=jnp.float32)
    left, middle, right = (product[:, c * channels : (c + 1) * channels] for c in range(3))
    if transposed:
        left, right = right, left
    return down(left, columns) + middle + up(right, columns)


def lay_taps(taps, kernel, transposed):
    c_in, c_out = kernel.shape[3:]
    for place, (a, b) in enumerate(TAPS):
        for c in range(3):
            if transposed:
                taps[c * c_in : (c + 1) * c_in, place * c_out : (place + 1) * c_out] = kernel[a, b, c]
            else:
                taps[place * c_in : (place + 1) * c_in, c * c_out : (c + 1) * c_out] = kernel[a, b, c]


def first_kernel(centre, time, near, far, corners, taps, slope, hidden, last, near_out, far_out, pad):
    lay(pad, centre, time, near, far, corners, False)
    frames, rows = centre.shape[:2]
    for t in range(frames):
        z = convolve(pad, taps, t, rows, False)
        s = jax.nn.sigmoid(z)
        slope[t] = (s * (1.0 + z * (1.0 - s))).reshape(slope.shape[1:])
        hidden[t] = (z * s).astype(jnp.bfloat16).reshape(hidden.shape[1:])
    strips(hidden, last, near_out, far_out, False)


def second_kernel(
    centre,
    time,
    near,
    far,
    corners,
    kernel,
    cotangent,
    output,
    grad,
    last,
    near_out,
    far_out,
    pad,
    taps,
    held,
    sems,
):
    lay(pad, centre, time, near, far, corners, False)
    lay_taps(taps, kernel, False)
    frames, rows = centre.shape[:2]
    for t in range(frames):
        z = convolve(pad, taps, t, rows, False)
        s = jax.nn.sigmoid(z)
        held[t] = (z * s).astype(jnp.bfloat16).reshape(held.shape[1:])
        pltpu.make_async_copy(held.at[t], output.at[t], sems.at[t]).start()
        steep = (s * (1.0 + z * (1.0 - s))).reshape(grad.shape[1:])
        grad[t] = (cotangent[t].astype(jnp.float32) * steep).astype(jnp.bfloat16)
    strips(grad, last, near_out, far_out, True)
    for t in range(frames):
        pltpu.make_async_copy(held.at[t], output.at[t], sems.at[t]).wait()


def back_kernel(centre, time, near, far, corners, kernel, grad, ended, pad, taps, held, sems):
    lay(pad, centre, time, near, far, corners, True)
    lay_taps(taps, kernel, True)
    frames, rows = centre.shape[:2]
    for t in range(frames):
        z = convolve(pad, taps, t, rows, True)
        held[t] = z.astype(jnp.bfloat16).reshape(held.shape[1:])
        pltpu.make_async_copy(held.at[t], grad.at[t], sems.at[t]).start()
    ended[...] = jnp.zeros_like(ended)
    for t in range(frames):
        pltpu.make_async_copy(held.at[t], grad.at[t], sems.at[t]).wait()


def back_slope_kernel(
    centre, time, near, far, corners, kernel, slope, grad, last, near_out, far_out, pad, taps
):
    lay(pad, centre, time, near, far, corners, True)
    lay_taps(taps, kernel, True)
    frames, rows = centre.shape[:2]
    for t in range(frames):
        z = convolve(pad, taps, t, rows, True).reshape(grad.shape[1:])
        grad[t] = (z * slope[t]).astype(jnp.bfloat16)
    strips(grad, last, near_out, far_out, True)


def weight_kernel(centre, time, near, far, corners, grad, keep, send, pad, moved):
    lay(pad, centre, time, near, far, corners, False)
    frames, rows, columns, channels = centre.shape
    cells = frames * rows * columns
    core = lax.axis_index("tm") % 2
    wide = grad[...].reshape(cells, channels).astype(jnp.float32)
    moved[:, :channels] = up(wide, columns).astype(jnp.bfloat16)
    moved[:, channels : 2 * channels] = grad[...].reshape(cells, channels)
    moved[:, 2 * channels :] = down(wide, columns).astype(jnp.bfloat16)
    dims = (((0,), (0,)), ((), ()))
    half = channels // 2
    for place, (a, b) in enumerate(TAPS):
        block = pad[a : a + frames, b : b + rows].reshape(cells, channels)
        product = lax.dot_general(block, moved[...], dims, preferred_element_type=jnp.float32)
        for c in range(3):
            part = product[:, c * channels : (c + 1) * channels]
            mine = jnp.where(core == 0, part[:half], part[half:])
            other = jnp.where(core == 0, part[half:], part[:half])
            keep[:, 3 * place + c] = mine.reshape(4, -1, channels)
            send[:, 3 * place + c] = other.astype(jnp.bfloat16).reshape(4, -1, channels)
    for out in (keep, send):
        out[:, 27:] = jnp.zeros_like(out[:, 27:])


def first_scatter_kernel(keep_one, came_one, keep_two, came_two, mine, *sent):
    x = lax.axis_index("height") % 4
    for d, out in enumerate((mine, *sent)):
        for k, (keep, came) in enumerate(((keep_one, came_one), (keep_two, came_two))):
            total = keep[x ^ d] + came[x ^ d].astype(jnp.float32)
            out[:, k] = total.reshape(4, -1, *total.shape[1:]).astype(out.dtype)


def second_scatter_kernel(own, one, two, three, mine, *sent):
    y = lax.axis_index("height") // 4
    for d, out in enumerate((mine, *sent)):
        own_part, *parts = (ref[y ^ d].astype(jnp.float32) for ref in (own, one, two, three))
        out[...] = ((own_part + parts[0]) + (parts[1] + parts[2])).astype(out.dtype)


def add_kernel(own, one, two, three, out):
    own, one, two, three = (ref[...].astype(jnp.float32) for ref in (own, one, two, three))
    out[...] = ((own + one) + (two + three)).astype(out.dtype)


def join_kernel(own, one, three, two, out):
    y = lax.axis_index("height") // 4
    for d, part in enumerate((own, one, two, three)):
        out[y ^ d] = part[...]


def gather_kernel(scale, *refs):
    pieces, outs, (held, sems) = refs[:8], refs[8:10], refs[10:]
    x, core = lax.axis_index("height") % 4, lax.axis_index("tm") % 2
    taps = outs[0].shape[0]
    copies = []
    for k, out in enumerate(outs):
        for q in range(4):
            first, count = 7 * q, min(7, taps - 7 * q)
            for d in range(4):
                for half in range(2):
                    block = pieces[4 * half + d][q, k, :count].astype(jnp.float32) * scale
                    held[k, pl.ds(first, count), pl.ds((core ^ half) * 4 + (x ^ d), 1)] = block[:, None]
            part = pl.ds(first, count)
            copies.append(pltpu.make_async_copy(held.at[k, part], out.at[part], sems.at[4 * k + q]))
            copies[-1].start()
    for copy in copies:
        copy.wait()


def swap(value, mask):
    return lax.ppermute(value, ALL, [(i, i ^ mask) for i in range(lax.axis_size(ALL))])


def kinds(shape):
    return [jax.ShapeDtypeStruct(shape, jnp.float32)] + 3 * [jax.ShapeDtypeStruct(shape, jnp.bfloat16)]


def started(one, two):
    _, taps, part, channels = one[0].shape
    shape = (4, 2, taps // 4, part, channels)
    halves = (one[0], swap(one[1], 16), two[0], swap(two[1], 16))
    return call(first_scatter_kernel, kinds(shape), [], 8 * math.prod(shape), *halves)


def summed(mine, sent, edged, ended):
    quarter = mine.shape[1:]
    size = math.prod(quarter)
    small = jax.ShapeDtypeStruct(quarter, jnp.bfloat16)
    one, two, three = (swap(value, d) for d, value in enumerate(sent, 1))
    mine, *sent = call(second_scatter_kernel, kinds(quarter), [], 16 * size, mine, two, one, three)
    one, two, three = (swap(value, 4 * d) for d, value in enumerate(sent, 1))
    (total,) = call(add_kernel, [small], [], 4 * size, mine, two, one, three, after=edged)
    one, two, three = (swap(total, mask) for mask in (64, 32, 96))
    (total,) = call(add_kernel, [small], [], 4 * size, total, one, three, two, after=ended)
    one, two, three = (swap(total, 4 * d) for d in (1, 2, 3))
    (total,) = call(
        join_kernel, [jax.ShapeDtypeStruct((4, *quarter), jnp.bfloat16)], [], 4 * size, total, one, three, two
    )
    return total


def spread(total, scale):
    part, channels = total.shape[3:]
    pieces = [total] + [swap(total, d) for d in (1, 2, 3)]
    pieces += [swap(value, 16) for value in pieces]
    whole = (27, 8, part, channels)
    outs = call(
        functools.partial(gather_kernel, scale),
        [jax.ShapeDtypeStruct(whole, jnp.float32)] * 2,
        [pltpu.VMEM((2, *whole), jnp.float32), pltpu.SemaphoreType.DMA((8,))],
        16 * total.size,
        *pieces,
        outside=(HBM, HBM),
    )
    return [out.reshape(3, 3, 3, channels, channels) for out in outs]


def time_route(ahead):
    count = lax.axis_size("tm")
    step = -1 if ahead else 1
    return [(i, (i + step) % count) for i in range(count)]


def pack_kernel(near, far, out, *, first):
    out[:, 0:1] = near[first : first + 2]
    out[:, 1:2] = far[first : first + 2]


def exchanged(last, near, far, ahead):
    line = lax.axis_size("height")
    time = lax.ppermute(last, "tm", time_route(ahead))
    near = lax.ppermute(near, "height", [(i, i ^ 1) for i in range(line)])
    far = lax.ppermute(far, "height", [(i, (i - 1 if i % 2 == 0 else i + 1) % line) for i in range(line)])
    return time, near, far


def cornered(time, near, far, ahead, after=()):
    shape = jax.ShapeDtypeStruct((2, 2, *near.shape[2:]), near.dtype)
    kernel = functools.partial(pack_kernel, first=0 if ahead else near.shape[0] - 2)
    if after:
        (rows,) = call(kernel, [shape], [], 0, near, far, after=after)
    else:
        rows = jnp.concatenate([near, far], axis=1)
        rows = rows[:2] if ahead else rows[-2:]
    return time, near, far, lax.ppermute(rows, "tm", time_route(ahead))


def body(clip, first_weight, second_weight, cotangent):
    _, frames, rows, columns, channels = clip.shape
    cells = frames * rows * columns
    clip, cotangent = clip[0], cotangent[0]
    flops = 2 * cells * 27 * channels * channels
    shape = (frames, rows, columns, channels)
    bf16 = jax.ShapeDtypeStruct(shape, jnp.bfloat16)
    f32 = jax.ShapeDtypeStruct(shape, jnp.float32)
    last = jax.ShapeDtypeStruct((2, *shape[1:]), jnp.bfloat16)
    line = jax.ShapeDtypeStruct((frames, 1, *shape[2:]), jnp.bfloat16)
    quarters = (4, 28, channels // 8, channels)
    keep = jax.ShapeDtypeStruct(quarters, jnp.float32)
    send = jax.ShapeDtypeStruct(quarters, jnp.bfloat16)
    pad = pltpu.VMEM((frames + 2, rows + 2, columns, channels), jnp.bfloat16)
    taps = pltpu.VMEM((9 * channels, 3 * channels), jnp.bfloat16)
    back_taps = pltpu.VMEM((3 * channels, 9 * channels), jnp.bfloat16)
    moved = pltpu.VMEM((cells, 3 * channels), jnp.bfloat16)
    out = pltpu.VMEM(shape, jnp.bfloat16), pltpu.SemaphoreType.DMA((frames,))
    scale = 1.0 / math.sqrt(cells * lax.axis_size(ALL))

    whole, *cut = call(
        cut_kernel, [bf16, last, line, line], [pltpu.SemaphoreType.DMA((4,))], 0, clip, inside=HBM
    )
    clip_edges = cornered(*exchanged(*cut, False), False)
    (first_taps,) = call(
        taps_kernel,
        [jax.ShapeDtypeStruct(taps.shape, taps.dtype)],
        [pltpu.VMEM(first_weight.shape, first_weight.dtype), pltpu.SemaphoreType.DMA((1,))],
        0,
        first_weight,
        inside=HBM,
    )
    slope, hidden, *cut = call(
        first_kernel, [f32, bf16, last, line, line], [pad], flops, whole, *clip_edges, first_taps
    )
    hidden_edges = cornered(*exchanged(*cut, False), False)
    output, grad_two, *cut = call(
        second_kernel,
        [bf16, bf16, last, line, line],
        [pad, taps, *out],
        flops,
        hidden,
        *hidden_edges,
        second_weight,
        cotangent,
        outside=(HBM,),
    )
    two_edges = cornered(*exchanged(*cut, True), True)
    second_terms = call(weight_kernel, [keep, send], [pad, moved], flops, hidden, *hidden_edges, grad_two)
    grad_one, *cut = call(
        back_slope_kernel,
        [bf16, last, line, line],
        [pad, back_taps],
        flops,
        grad_two,
        *two_edges,
        second_weight,
        slope,
    )
    one_edges = exchanged(*cut, True)
    first_terms = call(weight_kernel, [keep, send], [pad, moved], flops, whole, *clip_edges, grad_one)
    mine, *sent = started(first_terms, second_terms)
    one_edges = cornered(*one_edges, True, after=(mine,))
    ended = jax.ShapeDtypeStruct((8, 128), jnp.float32)
    clip_grad, ended = call(
        back_kernel,
        [bf16, ended],
        [pad, back_taps, *out],
        flops,
        grad_one,
        *one_edges,
        first_weight,
        outside=(HBM,),
    )
    first_grad, second_grad = spread(summed(mine, sent, (one_edges[0], one_edges[3]), (ended,)), scale)
    return output[None], clip_grad[None], first_grad, second_grad


def solution(mesh):
    block = P("dp", "tm", "height", None, None)
    return jax.shard_map(
        body,
        mesh=mesh,
        in_specs=(block, P(), P(), block),
        out_specs=(block, block, P(), P()),
        check_vma=False,
    )
```

```python
import functools
import math

import jax
import jax.numpy as jnp
from jax import lax
from jax.experimental import pallas as pl
from jax.experimental.pallas import tpu as pltpu
from jax.sharding import PartitionSpec as P

ALL = ("dp", "tm", "height")
PARAMS = pltpu.CompilerParams(vmem_limit_bytes=48 * 1024 * 1024)
VMEM = pl.BlockSpec(memory_space=pltpu.VMEM)
HBM = pl.BlockSpec(memory_space=pltpu.HBM)
ANY = pl.BlockSpec(memory_space=pl.ANY)
TAPS = [(a, b) for a in range(3) for b in range(3)]


def call(kernel, outs, scratch, flops, *args, after=(), inside=VMEM, outside=()):
    moved = sum(x.size * x.dtype.itemsize for x in (*args, *outs))

    def run(*refs):
        kernel(*refs[: len(args)], *refs[len(args) + len(after) :])

    return pl.pallas_call(
        run,
        out_shape=outs,
        in_specs=[inside] * len(args) + [ANY] * len(after),
        out_specs=list(outside) + [VMEM] * (len(outs) - len(outside)),
        scratch_shapes=scratch,
        compiler_params=PARAMS,
        cost_estimate=pl.CostEstimate(flops=flops, bytes_accessed=moved, transcendentals=0),
    )(*args, *after)


def copied(pairs, sems):
    copies = [pltpu.make_async_copy(source, target, sems.at[i]) for i, (source, target) in enumerate(pairs)]
    for copy in copies:
        copy.start()
    return copies


def cut_kernel(block, whole, last, near, far, sems):
    frames, rows = block.shape[:2]
    pairs = [
        (block.at[:, pl.ds(near_row(rows), 1)], near),
        (block.at[:, pl.ds(far_row(rows), 1)], far),
        (block.at[pl.ds(frames - 2, 2)], last),
        (block, whole),
    ]
    for copy in copied(pairs, sems):
        copy.wait()


def taps_kernel(kernel, taps, held, sems):
    (copy,) = copied([(kernel, held)], sems)
    copy.wait()
    lay_taps(taps, held, False)


def lay(pad, centre, time, near, far, corners, ahead):
    frames, rows = centre.shape[:2]
    place, above = near_row(rows + 2), far_row(rows + 2)
    own = pl.ds(0 if ahead else 2, frames)
    beyond = pl.ds(frames if ahead else 0, 2)
    pad[own, 1 : 1 + rows] = centre[...]
    pad[own, pl.ds(place, 1)] = near[...]
    pad[own, pl.ds(above, 1)] = far[...]
    pad[beyond, 1 : 1 + rows] = time[...]
    pad[beyond, pl.ds(place, 1)] = corners[:, 0:1]
    pad[beyond, pl.ds(above, 1)] = corners[:, 1:2]

    def clear(at):
        pad[at] = jnp.zeros_like(pad[at])

    line, tm = lax.axis_index("height"), lax.axis_index("tm")
    pl.when(line == 0)(lambda: clear((slice(None), slice(0, 1))))
    pl.when(line == lax.axis_size("height") - 1)(lambda: clear((slice(None), slice(rows + 1, rows + 2))))
    pl.when(tm == (lax.axis_size("tm") - 1 if ahead else 0))(lambda: clear((beyond,)))


def near_row(rows):
    return (1 - lax.axis_index("height") % 2) * (rows - 1)


def far_row(rows):
    return lax.axis_index("height") % 2 * (rows - 1)


def strips(block, last, near, far, ahead):
    frames, rows = block.shape[:2]
    last[...] = block[0:2] if ahead else block[frames - 2 :]
    near[...] = block[:, pl.ds(near_row(rows), 1)]
    far[...] = block[:, pl.ds(far_row(rows), 1)]


def down(value, columns):
    row = lax.broadcasted_iota(jnp.int32, value.shape, 0) % columns
    return jnp.where(row == 0, 0.0, pltpu.roll(value, 1, 0))


def up(value, columns):
    row = lax.broadcasted_iota(jnp.int32, value.shape, 0) % columns
    return jnp.where(row == columns - 1, 0.0, pltpu.roll(value, value.shape[0] - 1, 0))


def convolve(pad, taps, frame, rows, transposed):
    columns, channels = pad.shape[2:]
    parts = []
    for a, b in TAPS:
        t, h = (frame + 2 - a, 2 - b) if transposed else (frame + a, b)
        parts.append(pad[t, h : h + rows].reshape(rows * columns, channels))
    stacked = jnp.concatenate(parts, axis=1)
    dims = (((1,), (1 if transposed else 0,)), ((), ()))
    product = lax.dot_general(stacked, taps[...], dims, preferred_element_type=jnp.float32)
    left, middle, right = (product[:, c * channels : (c + 1) * channels] for c in range(3))
    if transposed:
        left, right = right, left
    return down(left, columns) + middle + up(right, columns)


def lay_taps(taps, kernel, transposed):
    c_in, c_out = kernel.shape[3:]
    for place, (a, b) in enumerate(TAPS):
        for c in range(3):
            if transposed:
                taps[c * c_in : (c + 1) * c_in, place * c_out : (place + 1) * c_out] = kernel[a, b, c]
            else:
                taps[place * c_in : (place + 1) * c_in, c * c_out : (c + 1) * c_out] = kernel[a, b, c]


def first_kernel(centre, time, near, far, corners, taps, slope, hidden, last, near_out, far_out, pad):
    lay(pad, centre, time, near, far, corners, False)
    frames, rows = centre.shape[:2]
    for t in range(frames):
        z = convolve(pad, taps, t, rows, False)
        s = jax.nn.sigmoid(z)
        slope[t] = (s * (1.0 + z * (1.0 - s))).reshape(slope.shape[1:])
        hidden[t] = (z * s).astype(jnp.bfloat16).reshape(hidden.shape[1:])
    strips(hidden, last, near_out, far_out, False)


def second_kernel(
    centre, time, near, far, corners, kernel, cotangent, output, grad, last, near_out, far_out, pad, taps
):
    lay(pad, centre, time, near, far, corners, False)
    lay_taps(taps, kernel, False)
    frames, rows = centre.shape[:2]
    for t in range(frames):
        z = convolve(pad, taps, t, rows, False)
        s = jax.nn.sigmoid(z)
        output[t] = (z * s).astype(jnp.bfloat16).reshape(output.shape[1:])
        steep = (s * (1.0 + z * (1.0 - s))).reshape(grad.shape[1:])
        grad[t] = (cotangent[t].astype(jnp.float32) * steep).astype(jnp.bfloat16)
    strips(grad, last, near_out, far_out, True)


def back_kernel(centre, time, near, far, corners, kernel, made, grad, output, ended, pad, taps, held, sems):
    frames, rows = centre.shape[:2]
    made_copy = pltpu.make_async_copy(made, output, sems.at[frames])
    made_copy.start()
    lay(pad, centre, time, near, far, corners, True)
    lay_taps(taps, kernel, True)
    for t in range(frames):
        z = convolve(pad, taps, t, rows, True)
        held[t] = z.astype(jnp.bfloat16).reshape(held.shape[1:])
        pltpu.make_async_copy(held.at[t], grad.at[t], sems.at[t]).start()
    ended[...] = jnp.zeros_like(ended)
    made_copy.wait()
    for t in range(frames):
        pltpu.make_async_copy(held.at[t], grad.at[t], sems.at[t]).wait()


def back_slope_kernel(
    centre, time, near, far, corners, kernel, slope, grad, last, near_out, far_out, pad, taps
):
    lay(pad, centre, time, near, far, corners, True)
    lay_taps(taps, kernel, True)
    frames, rows = centre.shape[:2]
    for t in range(frames):
        z = convolve(pad, taps, t, rows, True).reshape(grad.shape[1:])
        grad[t] = (z * slope[t]).astype(jnp.bfloat16)
    strips(grad, last, near_out, far_out, True)


def weight_kernel(centre, time, near, far, corners, grad, keep, send, pad, moved):
    lay(pad, centre, time, near, far, corners, False)
    frames, rows, columns, channels = centre.shape
    cells = frames * rows * columns
    core = lax.axis_index("tm") % 2
    wide = grad[...].reshape(cells, channels).astype(jnp.float32)
    moved[:, :channels] = up(wide, columns).astype(jnp.bfloat16)
    moved[:, channels : 2 * channels] = grad[...].reshape(cells, channels)
    moved[:, 2 * channels :] = down(wide, columns).astype(jnp.bfloat16)
    dims = (((0,), (0,)), ((), ()))
    half = channels // 2
    for place, (a, b) in enumerate(TAPS):
        block = pad[a : a + frames, b : b + rows].reshape(cells, channels)
        product = lax.dot_general(block, moved[...], dims, preferred_element_type=jnp.float32)
        for c in range(3):
            part = product[:, c * channels : (c + 1) * channels]
            mine = jnp.where(core == 0, part[:half], part[half:])
            other = jnp.where(core == 0, part[half:], part[:half])
            keep[:, 3 * place + c] = mine.reshape(4, -1, channels)
            send[:, 3 * place + c] = other.astype(jnp.bfloat16).reshape(4, -1, channels)
    for out in (keep, send):
        out[:, 27:] = jnp.zeros_like(out[:, 27:])


def scatter_kernel(keep_one, came_one, keep_two, came_two, mine, *parts):
    x = lax.axis_index("height") % 4
    over_one, over_three, plain_one, plain_three, later_one, later_three = parts
    targets = ((mine.at[0], plain_one, over_one, later_three), (mine.at[1], later_one, over_three, plain_three))
    for (keep, came), outs in zip(((keep_one, came_one), (keep_two, came_two)), targets, strict=True):
        for d in (2, 1, 3, 0):
            total = keep[x ^ d] + came[x ^ d].astype(jnp.float32)
            outs[d][...] = total.reshape(outs[d].shape).astype(outs[d].dtype)


def relay_kernel(later_one, later_three, came_one, came_three, to_one, to_three):
    to_one[...] = (later_one[...] + came_three[...].astype(jnp.float32)).astype(jnp.bfloat16)
    to_three[...] = (later_three[...] + came_one[...].astype(jnp.float32)).astype(jnp.bfloat16)


def second_scatter_kernel(own, one_first, three_first, one_second, three_second, mine, *sent):
    y = lax.axis_index("height") // 4
    for d, out in enumerate((mine, *sent)):
        for k, (one, three) in enumerate(((one_first, three_first), (one_second, three_second))):
            came = one[y ^ d].astype(jnp.float32) + three[y ^ d].astype(jnp.float32)
            out[k] = (own[k, y ^ d] + came).astype(out.dtype)


def add_kernel(own, one, two, three, out):
    own, one, two, three = (ref[...].astype(jnp.float32) for ref in (own, one, two, three))
    out[...] = ((own + one) + (two + three)).astype(out.dtype)


def join_kernel(own, one, three, two, out):
    y = lax.axis_index("height") // 4
    for d, part in enumerate((own, one, two, three)):
        out[:, y ^ d] = part[...]


def gather_kernel(scale, *refs):
    pieces, outs, (held, sems) = refs[:8], refs[8:10], refs[10:]
    x, core = lax.axis_index("height") % 4, lax.axis_index("tm") % 2
    taps = outs[0].shape[0]
    copies = []
    for k, out in enumerate(outs):
        for q in range(4):
            first, count = 7 * q, min(7, taps - 7 * q)
            for d in range(4):
                for half in range(2):
                    block = pieces[4 * half + d][k, q, :count].astype(jnp.float32) * scale
                    held[k, pl.ds(first, count), pl.ds((core ^ half) * 4 + (x ^ d), 1)] = block[:, None]
            part = pl.ds(first, count)
            copies.append(pltpu.make_async_copy(held.at[k, part], out.at[part], sems.at[4 * k + q]))
            copies[-1].start()
    for copy in copies:
        copy.wait()


def swap(value, mask):
    return lax.ppermute(value, ALL, [(i, i ^ mask) for i in range(lax.axis_size(ALL))])


def started(one, two):
    _, taps, part, channels = one[0].shape
    shape = (4, taps // 4, part, channels)
    f32 = jax.ShapeDtypeStruct((2, *shape), jnp.float32)
    bf16 = jax.ShapeDtypeStruct(shape, jnp.bfloat16)
    halves = (one[0], swap(one[1], 16), two[0], swap(two[1], 16))
    later = jax.ShapeDtypeStruct(shape, jnp.float32)
    return call(scatter_kernel, [f32, *4 * [bf16], later, later], [], 16 * math.prod(shape), *halves)


def summed(quarters, scale, cornered, ended):
    mine, over_one, over_three, plain_one, plain_three, *later = quarters
    shape = mine.shape
    part, channels = shape[3:]
    size = math.prod(shape)
    whole = jax.ShapeDtypeStruct(shape, jnp.bfloat16)
    half = jax.ShapeDtypeStruct(shape[1:], jnp.bfloat16)
    came = swap(over_one, 1), swap(over_three, 3)
    one_first, three_second = swap(plain_one, 1), swap(plain_three, 3)
    to_one, to_three = call(relay_kernel, [half, half], [], size, *later, *came)
    one_second, three_first = swap(to_one, 1), swap(to_three, 3)
    came = one_first, three_first, one_second, three_second
    quarter = (shape[0], *shape[2:])
    small = jax.ShapeDtypeStruct(quarter, jnp.bfloat16)
    exact = jax.ShapeDtypeStruct(quarter, jnp.float32)
    mine, *sent = call(
        second_scatter_kernel, [exact, small, small, small], [], 4 * size, mine, *came
    )
    one, two, three = (swap(value, 4 * d) for d, value in enumerate(sent, 1))
    (total,) = call(add_kernel, [small], [], size, mine, two, one, three, after=cornered)
    one, two, three = (swap(total, mask) for mask in (64, 32, 96))
    (total,) = call(add_kernel, [small], [], size, total, one, three, two, after=ended)
    one, two, three = (swap(total, 4 * d) for d in (1, 2, 3))
    (total,) = call(join_kernel, [whole], [], size, total, one, three, two)
    pieces = [total] + [swap(total, d) for d in (1, 2, 3)]
    pieces += [swap(value, 16) for value in pieces]
    out_shape = (27, 8, part, channels)
    outs = call(
        functools.partial(gather_kernel, scale),
        [jax.ShapeDtypeStruct(out_shape, jnp.float32)] * 2,
        [pltpu.VMEM((2, *out_shape), jnp.float32), pltpu.SemaphoreType.DMA((8,))],
        8 * size,
        *pieces,
        outside=(HBM, HBM),
    )
    return [out.reshape(3, 3, 3, channels, channels) for out in outs]


def time_route(ahead):
    count = lax.axis_size("tm")
    step = -1 if ahead else 1
    return [(i, (i + step) % count) for i in range(count)]


def pack_kernel(near, far, out, *, first):
    out[:, 0:1] = near[first : first + 2]
    out[:, 1:2] = far[first : first + 2]


def exchanged(last, near, far, ahead):
    line = lax.axis_size("height")
    time = lax.ppermute(last, "tm", time_route(ahead))
    near = lax.ppermute(near, "height", [(i, i ^ 1) for i in range(line)])
    far = lax.ppermute(far, "height", [(i, (i - 1 if i % 2 == 0 else i + 1) % line) for i in range(line)])
    return time, near, far


def cornered(time, near, far, ahead, after=()):
    shape = jax.ShapeDtypeStruct((2, 2, *near.shape[2:]), near.dtype)
    kernel = functools.partial(pack_kernel, first=0 if ahead else near.shape[0] - 2)
    if after:
        (rows,) = call(kernel, [shape], [], 0, near, far, after=after)
    else:
        rows = jnp.concatenate([near, far], axis=1)
        rows = rows[:2] if ahead else rows[-2:]
    return time, near, far, lax.ppermute(rows, "tm", time_route(ahead))


def body(clip, first_weight, second_weight, cotangent):
    _, frames, rows, columns, channels = clip.shape
    cells = frames * rows * columns
    clip, cotangent = clip[0], cotangent[0]
    flops = 2 * cells * 27 * channels * channels
    shape = (frames, rows, columns, channels)
    bf16 = jax.ShapeDtypeStruct(shape, jnp.bfloat16)
    f32 = jax.ShapeDtypeStruct(shape, jnp.float32)
    last = jax.ShapeDtypeStruct((2, *shape[1:]), jnp.bfloat16)
    line = jax.ShapeDtypeStruct((frames, 1, *shape[2:]), jnp.bfloat16)
    quarters = (4, 28, channels // 8, channels)
    keep = jax.ShapeDtypeStruct(quarters, jnp.float32)
    send = jax.ShapeDtypeStruct(quarters, jnp.bfloat16)
    pad = pltpu.VMEM((frames + 2, rows + 2, columns, channels), jnp.bfloat16)
    taps = pltpu.VMEM((9 * channels, 3 * channels), jnp.bfloat16)
    back_taps = pltpu.VMEM((3 * channels, 9 * channels), jnp.bfloat16)
    moved = pltpu.VMEM((cells, 3 * channels), jnp.bfloat16)
    out = pltpu.VMEM(shape, jnp.bfloat16), pltpu.SemaphoreType.DMA((frames + 1,))
    scale = 1.0 / math.sqrt(cells * lax.axis_size(ALL))

    whole, *cut = call(
        cut_kernel, [bf16, last, line, line], [pltpu.SemaphoreType.DMA((4,))], 0, clip, inside=HBM
    )
    clip_edges = cornered(*exchanged(*cut, False), False)
    (first_taps,) = call(
        taps_kernel,
        [jax.ShapeDtypeStruct(taps.shape, taps.dtype)],
        [pltpu.VMEM(first_weight.shape, first_weight.dtype), pltpu.SemaphoreType.DMA((1,))],
        0,
        first_weight,
        inside=HBM,
    )
    slope, hidden, *cut = call(
        first_kernel, [f32, bf16, last, line, line], [pad], flops, whole, *clip_edges, first_taps
    )
    hidden_edges = cornered(*exchanged(*cut, False), False)
    made, grad_two, *cut = call(
        second_kernel,
        [bf16, bf16, last, line, line],
        [pad, taps],
        flops,
        hidden,
        *hidden_edges,
        second_weight,
        cotangent,
    )
    two_edges = cornered(*exchanged(*cut, True), True)
    second_terms = call(weight_kernel, [keep, send], [pad, moved], flops, hidden, *hidden_edges, grad_two)
    grad_one, *cut = call(
        back_slope_kernel,
        [bf16, last, line, line],
        [pad, back_taps],
        flops,
        grad_two,
        *two_edges,
        second_weight,
        slope,
    )
    one_edges = exchanged(*cut, True)
    first_terms = call(weight_kernel, [keep, send], [pad, moved], flops, whole, *clip_edges, grad_one)
    quarters = started(first_terms, second_terms)
    one_edges = cornered(*one_edges, True, after=quarters[:1])
    ended = jax.ShapeDtypeStruct((8, 128), jnp.float32)
    clip_grad, output, ended = call(
        back_kernel,
        [bf16, bf16, ended],
        [pad, back_taps, *out],
        flops,
        grad_one,
        *one_edges,
        first_weight,
        made,
        outside=(HBM, HBM),
    )
    first_grad, second_grad = summed(quarters, scale, one_edges[3:], (ended,))
    return output[None], clip_grad[None], first_grad, second_grad


def solution(mesh):
    block = P("dp", "tm", "height", None, None)
    return jax.shard_map(
        body,
        mesh=mesh,
        in_specs=(block, P(), P(), block),
        out_specs=(block, block, P(), P()),
        check_vma=False,
    )
```

```python
import functools
import math

import jax
import jax.numpy as jnp
from jax import lax
from jax.experimental import pallas as pl
from jax.experimental.pallas import tpu as pltpu
from jax.sharding import PartitionSpec as P

ALL = ("dp", "tm", "height")
PARAMS = pltpu.CompilerParams(vmem_limit_bytes=48 * 1024 * 1024)
VMEM = pl.BlockSpec(memory_space=pltpu.VMEM)
HBM = pl.BlockSpec(memory_space=pltpu.HBM)
ANY = pl.BlockSpec(memory_space=pl.ANY)
TAPS = [(a, b) for a in range(3) for b in range(3)]


def call(kernel, outs, scratch, flops, *args, after=(), inside=VMEM, outside=()):
    moved = sum(x.size * x.dtype.itemsize for x in (*args, *outs))

    def run(*refs):
        kernel(*refs[: len(args)], *refs[len(args) + len(after) :])

    return pl.pallas_call(
        run,
        out_shape=outs,
        in_specs=[inside] * len(args) + [ANY] * len(after),
        out_specs=list(outside) + [VMEM] * (len(outs) - len(outside)),
        scratch_shapes=scratch,
        compiler_params=PARAMS,
        cost_estimate=pl.CostEstimate(flops=flops, bytes_accessed=moved, transcendentals=0),
    )(*args, *after)


def copied(pairs, sems):
    copies = [pltpu.make_async_copy(source, target, sems.at[i]) for i, (source, target) in enumerate(pairs)]
    for copy in copies:
        copy.start()
    return copies


def cut_kernel(block, whole, last, near, far, sems):
    frames, rows = block.shape[:2]
    pairs = [
        (block.at[:, pl.ds(near_row(rows), 1)], near),
        (block.at[:, pl.ds(far_row(rows), 1)], far),
        (block.at[pl.ds(frames - 2, 2)], last),
        (block, whole),
    ]
    for copy in copied(pairs, sems):
        copy.wait()


def taps_kernel(kernel, taps, held, sems):
    (copy,) = copied([(kernel, held)], sems)
    copy.wait()
    lay_taps(taps, held, False)


def lay(pad, centre, time, near, far, corners, ahead):
    frames, rows = centre.shape[:2]
    place, above = near_row(rows + 2), far_row(rows + 2)
    own = pl.ds(0 if ahead else 2, frames)
    beyond = pl.ds(frames if ahead else 0, 2)
    pad[own, 1 : 1 + rows] = centre[...]
    pad[own, pl.ds(place, 1)] = near[...]
    pad[own, pl.ds(above, 1)] = far[...]
    pad[beyond, 1 : 1 + rows] = time[...]
    pad[beyond, pl.ds(place, 1)] = corners[:, 0:1]
    pad[beyond, pl.ds(above, 1)] = corners[:, 1:2]

    def clear(at):
        pad[at] = jnp.zeros_like(pad[at])

    line, tm = lax.axis_index("height"), lax.axis_index("tm")
    pl.when(line == 0)(lambda: clear((slice(None), slice(0, 1))))
    pl.when(line == lax.axis_size("height") - 1)(lambda: clear((slice(None), slice(rows + 1, rows + 2))))
    pl.when(tm == (lax.axis_size("tm") - 1 if ahead else 0))(lambda: clear((beyond,)))


def near_row(rows):
    return (1 - lax.axis_index("height") % 2) * (rows - 1)


def far_row(rows):
    return lax.axis_index("height") % 2 * (rows - 1)


def strips(block, last, near, far, ahead):
    frames, rows = block.shape[:2]
    last[...] = block[0:2] if ahead else block[frames - 2 :]
    near[...] = block[:, pl.ds(near_row(rows), 1)]
    far[...] = block[:, pl.ds(far_row(rows), 1)]


def down(value, columns):
    row = lax.broadcasted_iota(jnp.int32, value.shape, 0) % columns
    return jnp.where(row == 0, 0.0, pltpu.roll(value, 1, 0))


def up(value, columns):
    row = lax.broadcasted_iota(jnp.int32, value.shape, 0) % columns
    return jnp.where(row == columns - 1, 0.0, pltpu.roll(value, value.shape[0] - 1, 0))


def convolve(pad, taps, frame, rows, transposed):
    columns, channels = pad.shape[2:]
    parts = []
    for a, b in TAPS:
        t, h = (frame + 2 - a, 2 - b) if transposed else (frame + a, b)
        parts.append(pad[t, h : h + rows].reshape(rows * columns, channels))
    stacked = jnp.concatenate(parts, axis=1)
    dims = (((1,), (1 if transposed else 0,)), ((), ()))
    product = lax.dot_general(stacked, taps[...], dims, preferred_element_type=jnp.float32)
    left, middle, right = (product[:, c * channels : (c + 1) * channels] for c in range(3))
    if transposed:
        left, right = right, left
    return down(left, columns) + middle + up(right, columns)


def lay_taps(taps, kernel, transposed):
    c_in, c_out = kernel.shape[3:]
    for place, (a, b) in enumerate(TAPS):
        for c in range(3):
            if transposed:
                taps[c * c_in : (c + 1) * c_in, place * c_out : (place + 1) * c_out] = kernel[a, b, c]
            else:
                taps[place * c_in : (place + 1) * c_in, c * c_out : (c + 1) * c_out] = kernel[a, b, c]


def first_kernel(centre, time, near, far, corners, taps, slope, hidden, last, near_out, far_out, pad):
    lay(pad, centre, time, near, far, corners, False)
    frames, rows = centre.shape[:2]
    for t in range(frames):
        z = convolve(pad, taps, t, rows, False)
        s = jax.nn.sigmoid(z)
        slope[t] = (s * (1.0 + z * (1.0 - s))).reshape(slope.shape[1:])
        hidden[t] = (z * s).astype(jnp.bfloat16).reshape(hidden.shape[1:])
    strips(hidden, last, near_out, far_out, False)


def second_kernel(
    centre, time, near, far, corners, kernel, cotangent, output, grad, last, near_out, far_out, pad, taps
):
    lay(pad, centre, time, near, far, corners, False)
    lay_taps(taps, kernel, False)
    frames, rows = centre.shape[:2]
    for t in range(frames):
        z = convolve(pad, taps, t, rows, False)
        s = jax.nn.sigmoid(z)
        output[t] = (z * s).astype(jnp.bfloat16).reshape(output.shape[1:])
        steep = (s * (1.0 + z * (1.0 - s))).reshape(grad.shape[1:])
        grad[t] = (cotangent[t].astype(jnp.float32) * steep).astype(jnp.bfloat16)
    strips(grad, last, near_out, far_out, True)


def back_kernel(centre, time, near, far, corners, kernel, made, output, grad, ended, pad, taps, sems):
    copy = pltpu.make_async_copy(made, output, sems.at[0])
    copy.start()
    lay(pad, centre, time, near, far, corners, True)
    lay_taps(taps, kernel, True)
    frames, rows = centre.shape[:2]
    for t in range(frames):
        z = convolve(pad, taps, t, rows, True)
        grad[t] = z.astype(jnp.bfloat16).reshape(grad.shape[1:])
    ended[...] = jnp.zeros_like(ended)
    copy.wait()


def back_slope_kernel(
    centre, time, near, far, corners, kernel, slope, grad, last, near_out, far_out, pad, taps
):
    lay(pad, centre, time, near, far, corners, True)
    lay_taps(taps, kernel, True)
    frames, rows = centre.shape[:2]
    for t in range(frames):
        z = convolve(pad, taps, t, rows, True).reshape(grad.shape[1:])
        grad[t] = (z * slope[t]).astype(jnp.bfloat16)
    strips(grad, last, near_out, far_out, True)


def weight_kernel(centre, time, near, far, corners, grad, keep, send, pad, moved):
    lay(pad, centre, time, near, far, corners, False)
    frames, rows, columns, channels = centre.shape
    cells = frames * rows * columns
    core = lax.axis_index("tm") % 2
    wide = grad[...].reshape(cells, channels).astype(jnp.float32)
    moved[:, :channels] = up(wide, columns).astype(jnp.bfloat16)
    moved[:, channels : 2 * channels] = grad[...].reshape(cells, channels)
    moved[:, 2 * channels :] = down(wide, columns).astype(jnp.bfloat16)
    dims = (((0,), (0,)), ((), ()))
    half = channels // 2
    for place, (a, b) in enumerate(TAPS):
        block = pad[a : a + frames, b : b + rows].reshape(cells, channels)
        product = lax.dot_general(block, moved[...], dims, preferred_element_type=jnp.float32)
        for c in range(3):
            part = product[:, c * channels : (c + 1) * channels]
            mine = jnp.where(core == 0, part[:half], part[half:])
            other = jnp.where(core == 0, part[half:], part[:half])
            keep[:, 3 * place + c] = mine.reshape(4, -1, channels)
            send[:, 3 * place + c] = other.astype(jnp.bfloat16).reshape(4, -1, channels)
    for out in (keep, send):
        out[:, 27:] = jnp.zeros_like(out[:, 27:])


def scatter_kernel(keep_one, came_one, keep_two, came_two, mine, *parts):
    x = lax.axis_index("height") % 4
    over_one, over_three, plain_one, plain_three, later_one, later_three = parts
    targets = ((mine.at[0], plain_one, over_one, later_three), (mine.at[1], later_one, over_three, plain_three))
    for (keep, came), outs in zip(((keep_one, came_one), (keep_two, came_two)), targets, strict=True):
        for d in (2, 1, 3, 0):
            total = keep[x ^ d] + came[x ^ d].astype(jnp.float32)
            outs[d][...] = total.reshape(outs[d].shape).astype(outs[d].dtype)


def relay_kernel(later_one, later_three, came_one, came_three, to_one, to_three):
    to_one[...] = (later_one[...] + came_three[...].astype(jnp.float32)).astype(jnp.bfloat16)
    to_three[...] = (later_three[...] + came_one[...].astype(jnp.float32)).astype(jnp.bfloat16)


def second_scatter_kernel(own, one_first, three_first, one_second, three_second, mine, *sent):
    y = lax.axis_index("height") // 4
    for d, out in enumerate((mine, *sent)):
        for k, (one, three) in enumerate(((one_first, three_first), (one_second, three_second))):
            came = one[y ^ d].astype(jnp.float32) + three[y ^ d].astype(jnp.float32)
            out[k] = (own[k, y ^ d] + came).astype(out.dtype)


def add_kernel(own, one, two, three, out):
    own, one, two, three = (ref[...].astype(jnp.float32) for ref in (own, one, two, three))
    out[...] = ((own + one) + (two + three)).astype(out.dtype)


def join_kernel(own, one, three, two, out):
    y = lax.axis_index("height") // 4
    for d, part in enumerate((own, one, two, three)):
        out[:, y ^ d] = part[...]


def gather_kernel(scale, *refs):
    pieces, made, outs, clip_grad, (held, sems) = refs[:8], refs[8], refs[9:11], refs[11], refs[12:]
    x, core = lax.axis_index("height") % 4, lax.axis_index("tm") % 2
    taps = outs[0].shape[0]
    copies = [pltpu.make_async_copy(made, clip_grad, sems.at[8])]
    copies[0].start()
    for k, out in enumerate(outs):
        for q in range(4):
            first, count = 7 * q, min(7, taps - 7 * q)
            for d in range(4):
                for half in range(2):
                    block = pieces[4 * half + d][k, q, :count].astype(jnp.float32) * scale
                    held[k, pl.ds(first, count), pl.ds((core ^ half) * 4 + (x ^ d), 1)] = block[:, None]
            part = pl.ds(first, count)
            copies.append(pltpu.make_async_copy(held.at[k, part], out.at[part], sems.at[4 * k + q]))
            copies[-1].start()
    for copy in copies:
        copy.wait()


def swap(value, mask):
    return lax.ppermute(value, ALL, [(i, i ^ mask) for i in range(lax.axis_size(ALL))])


def started(one, two):
    _, taps, part, channels = one[0].shape
    shape = (4, taps // 4, part, channels)
    f32 = jax.ShapeDtypeStruct((2, *shape), jnp.float32)
    bf16 = jax.ShapeDtypeStruct(shape, jnp.bfloat16)
    halves = (one[0], swap(one[1], 16), two[0], swap(two[1], 16))
    later = jax.ShapeDtypeStruct(shape, jnp.float32)
    return call(scatter_kernel, [f32, *4 * [bf16], later, later], [], 16 * math.prod(shape), *halves)


def summed(quarters, scale, cornered, ended, made):
    mine, over_one, over_three, plain_one, plain_three, *later = quarters
    shape = mine.shape
    part, channels = shape[3:]
    size = math.prod(shape)
    whole = jax.ShapeDtypeStruct(shape, jnp.bfloat16)
    half = jax.ShapeDtypeStruct(shape[1:], jnp.bfloat16)
    came = swap(over_one, 1), swap(over_three, 3)
    one_first, three_second = swap(plain_one, 1), swap(plain_three, 3)
    to_one, to_three = call(relay_kernel, [half, half], [], size, *later, *came)
    one_second, three_first = swap(to_one, 1), swap(to_three, 3)
    came = one_first, three_first, one_second, three_second
    quarter = (shape[0], *shape[2:])
    small = jax.ShapeDtypeStruct(quarter, jnp.bfloat16)
    exact = jax.ShapeDtypeStruct(quarter, jnp.float32)
    mine, *sent = call(
        second_scatter_kernel, [exact, small, small, small], [], 4 * size, mine, *came
    )
    one, two, three = (swap(value, 4 * d) for d, value in enumerate(sent, 1))
    (total,) = call(add_kernel, [small], [], size, mine, two, one, three, after=cornered)
    one, two, three = (swap(total, mask) for mask in (64, 32, 96))
    (total,) = call(add_kernel, [small], [], size, total, one, three, two, after=ended)
    one, two, three = (swap(total, 4 * d) for d in (1, 2, 3))
    (total,) = call(join_kernel, [whole], [], size, total, one, three, two)
    pieces = [total] + [swap(total, d) for d in (1, 2, 3)]
    pieces += [swap(value, 16) for value in pieces]
    out_shape = (27, 8, part, channels)
    outs = call(
        functools.partial(gather_kernel, scale),
        [jax.ShapeDtypeStruct(out_shape, jnp.float32)] * 2 + [jax.ShapeDtypeStruct(made.shape, made.dtype)],
        [pltpu.VMEM((2, *out_shape), jnp.float32), pltpu.SemaphoreType.DMA((9,))],
        8 * size,
        *pieces,
        made,
        outside=(HBM, HBM, HBM),
    )
    return [out.reshape(3, 3, 3, channels, channels) for out in outs[:2]] + list(outs[2:])


def time_route(ahead):
    count = lax.axis_size("tm")
    step = -1 if ahead else 1
    return [(i, (i + step) % count) for i in range(count)]


def pack_kernel(near, far, out, *, first):
    out[:, 0:1] = near[first : first + 2]
    out[:, 1:2] = far[first : first + 2]


def exchanged(last, near, far, ahead):
    line = lax.axis_size("height")
    time = lax.ppermute(last, "tm", time_route(ahead))
    near = lax.ppermute(near, "height", [(i, i ^ 1) for i in range(line)])
    far = lax.ppermute(far, "height", [(i, (i - 1 if i % 2 == 0 else i + 1) % line) for i in range(line)])
    return time, near, far


def cornered(time, near, far, ahead, after=()):
    shape = jax.ShapeDtypeStruct((2, 2, *near.shape[2:]), near.dtype)
    kernel = functools.partial(pack_kernel, first=0 if ahead else near.shape[0] - 2)
    if after:
        (rows,) = call(kernel, [shape], [], 0, near, far, after=after)
    else:
        rows = jnp.concatenate([near, far], axis=1)
        rows = rows[:2] if ahead else rows[-2:]
    return time, near, far, lax.ppermute(rows, "tm", time_route(ahead))


def body(clip, first_weight, second_weight, cotangent):
    _, frames, rows, columns, channels = clip.shape
    cells = frames * rows * columns
    clip, cotangent = clip[0], cotangent[0]
    flops = 2 * cells * 27 * channels * channels
    shape = (frames, rows, columns, channels)
    bf16 = jax.ShapeDtypeStruct(shape, jnp.bfloat16)
    f32 = jax.ShapeDtypeStruct(shape, jnp.float32)
    last = jax.ShapeDtypeStruct((2, *shape[1:]), jnp.bfloat16)
    line = jax.ShapeDtypeStruct((frames, 1, *shape[2:]), jnp.bfloat16)
    quarters = (4, 28, channels // 8, channels)
    keep = jax.ShapeDtypeStruct(quarters, jnp.float32)
    send = jax.ShapeDtypeStruct(quarters, jnp.bfloat16)
    pad = pltpu.VMEM((frames + 2, rows + 2, columns, channels), jnp.bfloat16)
    taps = pltpu.VMEM((9 * channels, 3 * channels), jnp.bfloat16)
    back_taps = pltpu.VMEM((3 * channels, 9 * channels), jnp.bfloat16)
    moved = pltpu.VMEM((cells, 3 * channels), jnp.bfloat16)
    scale = 1.0 / math.sqrt(cells * lax.axis_size(ALL))

    whole, *cut = call(
        cut_kernel, [bf16, last, line, line], [pltpu.SemaphoreType.DMA((4,))], 0, clip, inside=HBM
    )
    clip_edges = cornered(*exchanged(*cut, False), False)
    (first_taps,) = call(
        taps_kernel,
        [jax.ShapeDtypeStruct(taps.shape, taps.dtype)],
        [pltpu.VMEM(first_weight.shape, first_weight.dtype), pltpu.SemaphoreType.DMA((1,))],
        0,
        first_weight,
        inside=HBM,
    )
    slope, hidden, *cut = call(
        first_kernel, [f32, bf16, last, line, line], [pad], flops, whole, *clip_edges, first_taps
    )
    hidden_edges = cornered(*exchanged(*cut, False), False)
    made, grad_two, *cut = call(
        second_kernel,
        [bf16, bf16, last, line, line],
        [pad, taps],
        flops,
        hidden,
        *hidden_edges,
        second_weight,
        cotangent,
    )
    two_edges = cornered(*exchanged(*cut, True), True)
    second_terms = call(weight_kernel, [keep, send], [pad, moved], flops, hidden, *hidden_edges, grad_two)
    grad_one, *cut = call(
        back_slope_kernel,
        [bf16, last, line, line],
        [pad, back_taps],
        flops,
        grad_two,
        *two_edges,
        second_weight,
        slope,
    )
    one_edges = exchanged(*cut, True)
    first_terms = call(weight_kernel, [keep, send], [pad, moved], flops, whole, *clip_edges, grad_one)
    quarters = started(first_terms, second_terms)
    one_edges = cornered(*one_edges, True, after=quarters[:1])
    ended = jax.ShapeDtypeStruct((8, 128), jnp.float32)
    output, grad, ended = call(
        back_kernel,
        [bf16, bf16, ended],
        [pad, back_taps, pltpu.SemaphoreType.DMA((1,))],
        flops,
        grad_one,
        *one_edges,
        first_weight,
        made,
        outside=(HBM,),
    )
    first_grad, second_grad, clip_grad = summed(quarters, scale, one_edges[3:], (ended,), grad)
    return output[None], clip_grad[None], first_grad, second_grad


def solution(mesh):
    block = P("dp", "tm", "height", None, None)
    return jax.shard_map(
        body,
        mesh=mesh,
        in_specs=(block, P(), P(), block),
        out_specs=(block, block, P(), P()),
        check_vma=False,
    )
```

```python
import functools
import math

import jax
import jax.numpy as jnp
from jax import lax
from jax.experimental import pallas as pl
from jax.experimental.pallas import tpu as pltpu
from jax.sharding import PartitionSpec as P

ALL = ("dp", "tm", "height")
PARAMS = pltpu.CompilerParams(vmem_limit_bytes=48 * 1024 * 1024)
VMEM = pl.BlockSpec(memory_space=pltpu.VMEM)
HBM = pl.BlockSpec(memory_space=pltpu.HBM)
ANY = pl.BlockSpec(memory_space=pl.ANY)
TAPS = [(a, b) for a in range(3) for b in range(3)]


def call(kernel, outs, scratch, flops, *args, after=(), inside=VMEM, outside=()):
    moved = sum(x.size * x.dtype.itemsize for x in (*args, *outs))

    def run(*refs):
        kernel(*refs[: len(args)], *refs[len(args) + len(after) :])

    return pl.pallas_call(
        run,
        out_shape=outs,
        in_specs=[inside] * len(args) + [ANY] * len(after),
        out_specs=list(outside) + [VMEM] * (len(outs) - len(outside)),
        scratch_shapes=scratch,
        compiler_params=PARAMS,
        cost_estimate=pl.CostEstimate(flops=flops, bytes_accessed=moved, transcendentals=0),
    )(*args, *after)


def copied(pairs, sems):
    copies = [pltpu.make_async_copy(source, target, sems.at[i]) for i, (source, target) in enumerate(pairs)]
    for copy in copies:
        copy.start()
    return copies


def cut_kernel(block, whole, last, near, far, sems):
    frames, rows = block.shape[:2]
    pairs = [
        (block.at[:, pl.ds(near_row(rows), 1)], near),
        (block.at[:, pl.ds(far_row(rows), 1)], far),
        (block.at[pl.ds(frames - 2, 2)], last),
        (block, whole),
    ]
    for copy in copied(pairs, sems):
        copy.wait()


def taps_kernel(kernel, taps, held, sems):
    (copy,) = copied([(kernel, held)], sems)
    copy.wait()
    lay_taps(taps, held, False)


def lay(pad, centre, time, near, far, corners, ahead):
    frames, rows = centre.shape[:2]
    place, above = near_row(rows + 2), far_row(rows + 2)
    own = pl.ds(0 if ahead else 2, frames)
    beyond = pl.ds(frames if ahead else 0, 2)
    pad[own, 1 : 1 + rows] = centre[...]
    pad[own, pl.ds(place, 1)] = near[...]
    pad[own, pl.ds(above, 1)] = far[...]
    pad[beyond, 1 : 1 + rows] = time[...]
    pad[beyond, pl.ds(place, 1)] = corners[:, 0:1]
    pad[beyond, pl.ds(above, 1)] = corners[:, 1:2]

    def clear(at):
        pad[at] = jnp.zeros_like(pad[at])

    line, tm = lax.axis_index("height"), lax.axis_index("tm")
    pl.when(line == 0)(lambda: clear((slice(None), slice(0, 1))))
    pl.when(line == lax.axis_size("height") - 1)(lambda: clear((slice(None), slice(rows + 1, rows + 2))))
    pl.when(tm == (lax.axis_size("tm") - 1 if ahead else 0))(lambda: clear((beyond,)))


def near_row(rows):
    return (1 - lax.axis_index("height") % 2) * (rows - 1)


def far_row(rows):
    return lax.axis_index("height") % 2 * (rows - 1)


def strips(block, last, near, far, ahead):
    frames, rows = block.shape[:2]
    last[...] = block[0:2] if ahead else block[frames - 2 :]
    near[...] = block[:, pl.ds(near_row(rows), 1)]
    far[...] = block[:, pl.ds(far_row(rows), 1)]


def down(value, columns):
    row = lax.broadcasted_iota(jnp.int32, value.shape, 0) % columns
    return jnp.where(row == 0, 0.0, pltpu.roll(value, 1, 0))


def up(value, columns):
    row = lax.broadcasted_iota(jnp.int32, value.shape, 0) % columns
    return jnp.where(row == columns - 1, 0.0, pltpu.roll(value, value.shape[0] - 1, 0))


def convolve(pad, taps, frame, row, rows, transposed):
    columns, channels = pad.shape[2:]
    parts = []
    for a, b in TAPS:
        t, h = (frame + 2 - a, row + 2 - b) if transposed else (frame + a, row + b)
        parts.append(pad[t, h : h + rows].reshape(rows * columns, channels))
    stacked = jnp.concatenate(parts, axis=1)
    dims = (((1,), (1 if transposed else 0,)), ((), ()))
    product = lax.dot_general(stacked, taps[...], dims, preferred_element_type=jnp.float32)
    left, middle, right = (product[:, c * channels : (c + 1) * channels] for c in range(3))
    if transposed:
        left, right = right, left
    return down(left, columns) + middle + up(right, columns)


def lay_taps(taps, kernel, transposed):
    c_in, c_out = kernel.shape[3:]
    for place, (a, b) in enumerate(TAPS):
        for c in range(3):
            if transposed:
                taps[c * c_in : (c + 1) * c_in, place * c_out : (place + 1) * c_out] = kernel[a, b, c]
            else:
                taps[place * c_in : (place + 1) * c_in, c * c_out : (c + 1) * c_out] = kernel[a, b, c]


def blocks(frames, rows):
    return [(t, slice(h, h + 2)) for t in range(frames) for h in range(0, rows, 2)]


def first_kernel(centre, time, near, far, corners, taps, slope, hidden, last, near_out, far_out, pad):
    lay(pad, centre, time, near, far, corners, False)
    frames, rows = centre.shape[:2]
    for t, rows in blocks(frames, rows):
        z = convolve(pad, taps, t, rows.start, 2, False)
        s = jax.nn.sigmoid(z)
        slope[t, rows] = (s * (1.0 + z * (1.0 - s))).reshape(2, *slope.shape[2:])
        hidden[t, rows] = (z * s).astype(jnp.bfloat16).reshape(2, *hidden.shape[2:])
    strips(hidden, last, near_out, far_out, False)


def second_kernel(
    centre, time, near, far, corners, kernel, cotangent, output, grad, last, near_out, far_out, pad, taps
):
    lay(pad, centre, time, near, far, corners, False)
    lay_taps(taps, kernel, False)
    frames, rows = centre.shape[:2]
    for t, rows in blocks(frames, rows):
        z = convolve(pad, taps, t, rows.start, 2, False)
        s = jax.nn.sigmoid(z)
        output[t, rows] = (z * s).astype(jnp.bfloat16).reshape(2, *output.shape[2:])
        steep = (s * (1.0 + z * (1.0 - s))).reshape(2, *grad.shape[2:])
        grad[t, rows] = (cotangent[t, rows].astype(jnp.float32) * steep).astype(jnp.bfloat16)
    strips(grad, last, near_out, far_out, True)


def back_kernel(centre, time, near, far, corners, kernel, made, output, grad, ended, pad, taps, sems):
    copy = pltpu.make_async_copy(made, output, sems.at[0])
    copy.start()
    lay(pad, centre, time, near, far, corners, True)
    lay_taps(taps, kernel, True)
    frames, rows = centre.shape[:2]
    for t, rows in blocks(frames, rows):
        z = convolve(pad, taps, t, rows.start, 2, True)
        grad[t, rows] = z.astype(jnp.bfloat16).reshape(2, *grad.shape[2:])
    ended[...] = jnp.zeros_like(ended)
    copy.wait()


def back_slope_kernel(
    centre, time, near, far, corners, kernel, slope, grad, last, near_out, far_out, pad, taps
):
    lay(pad, centre, time, near, far, corners, True)
    lay_taps(taps, kernel, True)
    frames, rows = centre.shape[:2]
    for t, rows in blocks(frames, rows):
        z = convolve(pad, taps, t, rows.start, 2, True).reshape(2, *grad.shape[2:])
        grad[t, rows] = (z * slope[t, rows]).astype(jnp.bfloat16)
    strips(grad, last, near_out, far_out, True)


def weight_kernel(centre, time, near, far, corners, grad, keep, send, pad, moved):
    lay(pad, centre, time, near, far, corners, False)
    frames, rows, columns, channels = centre.shape
    cells = frames * rows * columns
    core = lax.axis_index("tm") % 2
    wide = grad[...].reshape(cells, channels).astype(jnp.float32)
    moved[:, :channels] = up(wide, columns).astype(jnp.bfloat16)
    moved[:, channels : 2 * channels] = grad[...].reshape(cells, channels)
    moved[:, 2 * channels :] = down(wide, columns).astype(jnp.bfloat16)
    dims = (((0,), (0,)), ((), ()))
    half = channels // 2
    for place, (a, b) in enumerate(TAPS):
        block = pad[a : a + frames, b : b + rows].reshape(cells, channels)
        product = lax.dot_general(block, moved[...], dims, preferred_element_type=jnp.float32)
        for c in range(3):
            part = product[:, c * channels : (c + 1) * channels]
            mine = jnp.where(core == 0, part[:half], part[half:])
            other = jnp.where(core == 0, part[half:], part[:half])
            keep[:, 3 * place + c] = mine.reshape(4, -1, channels)
            send[:, 3 * place + c] = other.astype(jnp.bfloat16).reshape(4, -1, channels)
    for out in (keep, send):
        out[:, 27:] = jnp.zeros_like(out[:, 27:])


def scatter_kernel(keep_one, came_one, keep_two, came_two, mine, *parts):
    x = lax.axis_index("height") % 4
    over_one, over_three, plain_one, plain_three, later_one, later_three = parts
    targets = ((mine.at[0], plain_one, over_one, later_three), (mine.at[1], later_one, over_three, plain_three))
    for (keep, came), outs in zip(((keep_one, came_one), (keep_two, came_two)), targets, strict=True):
        for d in (2, 1, 3, 0):
            total = keep[x ^ d] + came[x ^ d].astype(jnp.float32)
            outs[d][...] = total.reshape(outs[d].shape).astype(outs[d].dtype)


def relay_kernel(later_one, later_three, came_one, came_three, to_one, to_three):
    to_one[...] = (later_one[...] + came_three[...].astype(jnp.float32)).astype(jnp.bfloat16)
    to_three[...] = (later_three[...] + came_one[...].astype(jnp.float32)).astype(jnp.bfloat16)


def second_scatter_kernel(own, one_first, three_first, one_second, three_second, mine, *sent):
    y = lax.axis_index("height") // 4
    for d, out in enumerate((mine, *sent)):
        for k, (one, three) in enumerate(((one_first, three_first), (one_second, three_second))):
            came = one[y ^ d].astype(jnp.float32) + three[y ^ d].astype(jnp.float32)
            out[k] = (own[k, y ^ d] + came).astype(out.dtype)


def add_kernel(own, one, two, three, out):
    own, one, two, three = (ref[...].astype(jnp.float32) for ref in (own, one, two, three))
    out[...] = ((own + one) + (two + three)).astype(out.dtype)


def join_kernel(own, one, three, two, out):
    y = lax.axis_index("height") // 4
    for d, part in enumerate((own, one, two, three)):
        out[:, y ^ d] = part[...]


def gather_kernel(scale, *refs):
    pieces, made, outs, clip_grad, (held, sems) = refs[:8], refs[8], refs[9:11], refs[11], refs[12:]
    x, core = lax.axis_index("height") % 4, lax.axis_index("tm") % 2
    taps = outs[0].shape[0]
    copies = [pltpu.make_async_copy(made, clip_grad, sems.at[8])]
    copies[0].start()
    for k, out in enumerate(outs):
        for q in range(4):
            first, count = 7 * q, min(7, taps - 7 * q)
            for place, d in enumerate((0, 1, 3, 2)):
                for half in range(2):
                    block = pieces[4 * half + place][k, q, :count].astype(jnp.float32) * scale
                    held[k, pl.ds(first, count), pl.ds((core ^ half) * 4 + (x ^ d), 1)] = block[:, None]
            part = pl.ds(first, count)
            copies.append(pltpu.make_async_copy(held.at[k, part], out.at[part], sems.at[4 * k + q]))
            copies[-1].start()
    for copy in copies:
        copy.wait()


def swap(value, mask):
    return lax.ppermute(value, ALL, [(i, i ^ mask) for i in range(lax.axis_size(ALL))])


def started(one, two):
    _, taps, part, channels = one[0].shape
    shape = (4, taps // 4, part, channels)
    f32 = jax.ShapeDtypeStruct((2, *shape), jnp.float32)
    bf16 = jax.ShapeDtypeStruct(shape, jnp.bfloat16)
    halves = (one[0], swap(one[1], 16), two[0], swap(two[1], 16))
    later = jax.ShapeDtypeStruct(shape, jnp.float32)
    return call(scatter_kernel, [f32, *4 * [bf16], later, later], [], 16 * math.prod(shape), *halves)


def summed(quarters, scale, cornered, ended, made):
    mine, over_one, over_three, plain_one, plain_three, *later = quarters
    shape = mine.shape
    part, channels = shape[3:]
    size = math.prod(shape)
    whole = jax.ShapeDtypeStruct(shape, jnp.bfloat16)
    half = jax.ShapeDtypeStruct(shape[1:], jnp.bfloat16)
    came = swap(over_one, 1), swap(over_three, 3)
    one_first, three_second = swap(plain_one, 1), swap(plain_three, 3)
    to_one, to_three = call(relay_kernel, [half, half], [], size, *later, *came)
    one_second, three_first = swap(to_one, 1), swap(to_three, 3)
    came = one_first, three_first, one_second, three_second
    quarter = (shape[0], *shape[2:])
    small = jax.ShapeDtypeStruct(quarter, jnp.bfloat16)
    exact = jax.ShapeDtypeStruct(quarter, jnp.float32)
    mine, *sent = call(
        second_scatter_kernel, [exact, small, small, small], [], 4 * size, mine, *came
    )
    one, two, three = (swap(value, 4 * d) for d, value in enumerate(sent, 1))
    (total,) = call(add_kernel, [small], [], size, mine, two, one, three, after=cornered)
    one, two, three = (swap(total, mask) for mask in (64, 32, 96))
    (total,) = call(add_kernel, [small], [], size, total, one, three, two, after=ended)
    one, two, three = (swap(total, 4 * d) for d in (1, 2, 3))
    (total,) = call(join_kernel, [whole], [], size, total, one, three, two)
    pieces = [total] + [swap(total, d) for d in (1, 3, 2)]
    pieces += [swap(value, 16) for value in pieces]
    out_shape = (27, 8, part, channels)
    outs = call(
        functools.partial(gather_kernel, scale),
        [jax.ShapeDtypeStruct(out_shape, jnp.float32)] * 2 + [jax.ShapeDtypeStruct(made.shape, made.dtype)],
        [pltpu.VMEM((2, *out_shape), jnp.float32), pltpu.SemaphoreType.DMA((9,))],
        8 * size,
        *pieces,
        made,
        outside=(HBM, HBM, HBM),
    )
    return [out.reshape(3, 3, 3, channels, channels) for out in outs[:2]] + list(outs[2:])


def time_route(ahead):
    count = lax.axis_size("tm")
    step = -1 if ahead else 1
    return [(i, (i + step) % count) for i in range(count)]


def pack_kernel(near, far, out, *, first):
    out[:, 0:1] = near[first : first + 2]
    out[:, 1:2] = far[first : first + 2]


def exchanged(last, near, far, ahead):
    line = lax.axis_size("height")
    time = lax.ppermute(last, "tm", time_route(ahead))
    near = lax.ppermute(near, "height", [(i, i ^ 1) for i in range(line)])
    far = lax.ppermute(far, "height", [(i, (i - 1 if i % 2 == 0 else i + 1) % line) for i in range(line)])
    return time, near, far


def cornered(time, near, far, ahead, after=()):
    shape = jax.ShapeDtypeStruct((2, 2, *near.shape[2:]), near.dtype)
    kernel = functools.partial(pack_kernel, first=0 if ahead else near.shape[0] - 2)
    if after:
        (rows,) = call(kernel, [shape], [], 0, near, far, after=after)
    else:
        rows = jnp.concatenate([near, far], axis=1)
        rows = rows[:2] if ahead else rows[-2:]
    return time, near, far, lax.ppermute(rows, "tm", time_route(ahead))


def body(clip, first_weight, second_weight, cotangent):
    _, frames, rows, columns, channels = clip.shape
    cells = frames * rows * columns
    clip, cotangent = clip[0], cotangent[0]
    flops = 2 * cells * 27 * channels * channels
    shape = (frames, rows, columns, channels)
    bf16 = jax.ShapeDtypeStruct(shape, jnp.bfloat16)
    f32 = jax.ShapeDtypeStruct(shape, jnp.float32)
    last = jax.ShapeDtypeStruct((2, *shape[1:]), jnp.bfloat16)
    line = jax.ShapeDtypeStruct((frames, 1, *shape[2:]), jnp.bfloat16)
    quarters = (4, 28, channels // 8, channels)
    keep = jax.ShapeDtypeStruct(quarters, jnp.float32)
    send = jax.ShapeDtypeStruct(quarters, jnp.bfloat16)
    pad = pltpu.VMEM((frames + 2, rows + 2, columns, channels), jnp.bfloat16)
    taps = pltpu.VMEM((9 * channels, 3 * channels), jnp.bfloat16)
    back_taps = pltpu.VMEM((3 * channels, 9 * channels), jnp.bfloat16)
    moved = pltpu.VMEM((cells, 3 * channels), jnp.bfloat16)
    scale = 1.0 / math.sqrt(cells * lax.axis_size(ALL))

    whole, *cut = call(
        cut_kernel, [bf16, last, line, line], [pltpu.SemaphoreType.DMA((4,))], 0, clip, inside=HBM
    )
    clip_edges = cornered(*exchanged(*cut, False), False)
    (first_taps,) = call(
        taps_kernel,
        [jax.ShapeDtypeStruct(taps.shape, taps.dtype)],
        [pltpu.VMEM(first_weight.shape, first_weight.dtype), pltpu.SemaphoreType.DMA((1,))],
        0,
        first_weight,
        inside=HBM,
    )
    slope, hidden, *cut = call(
        first_kernel, [f32, bf16, last, line, line], [pad], flops, whole, *clip_edges, first_taps
    )
    hidden_edges = cornered(*exchanged(*cut, False), False)
    made, grad_two, *cut = call(
        second_kernel,
        [bf16, bf16, last, line, line],
        [pad, taps],
        flops,
        hidden,
        *hidden_edges,
        second_weight,
        cotangent,
    )
    two_edges = cornered(*exchanged(*cut, True), True)
    second_terms = call(weight_kernel, [keep, send], [pad, moved], flops, hidden, *hidden_edges, grad_two)
    grad_one, *cut = call(
        back_slope_kernel,
        [bf16, last, line, line],
        [pad, back_taps],
        flops,
        grad_two,
        *two_edges,
        second_weight,
        slope,
    )
    one_edges = exchanged(*cut, True)
    first_terms = call(weight_kernel, [keep, send], [pad, moved], flops, whole, *clip_edges, grad_one)
    quarters = started(first_terms, second_terms)
    one_edges = cornered(*one_edges, True, after=quarters[:1])
    ended = jax.ShapeDtypeStruct((8, 128), jnp.float32)
    output, grad, ended = call(
        back_kernel,
        [bf16, bf16, ended],
        [pad, back_taps, pltpu.SemaphoreType.DMA((1,))],
        flops,
        grad_one,
        *one_edges,
        first_weight,
        made,
        outside=(HBM,),
    )
    first_grad, second_grad, clip_grad = summed(quarters, scale, one_edges[3:], (ended,), grad)
    return output[None], clip_grad[None], first_grad, second_grad


def solution(mesh):
    block = P("dp", "tm", "height", None, None)
    return jax.shard_map(
        body,
        mesh=mesh,
        in_specs=(block, P(), P(), block),
        out_specs=(block, block, P(), P()),
        check_vma=False,
    )
```

```python
import functools
import math

import jax
import jax.numpy as jnp
from jax import lax
from jax.experimental import pallas as pl
from jax.experimental.pallas import tpu as pltpu
from jax.sharding import PartitionSpec as P

ALL = ("dp", "tm", "height")
PARAMS = pltpu.CompilerParams(vmem_limit_bytes=48 * 1024 * 1024)
VMEM = pl.BlockSpec(memory_space=pltpu.VMEM)
HBM = pl.BlockSpec(memory_space=pltpu.HBM)
ANY = pl.BlockSpec(memory_space=pl.ANY)
TAPS = [(a, b) for a in range(3) for b in range(3)]


def call(kernel, outs, scratch, flops, *args, after=(), inside=VMEM, outside=()):
    moved = sum(x.size * x.dtype.itemsize for x in (*args, *outs))

    def run(*refs):
        kernel(*refs[: len(args)], *refs[len(args) + len(after) :])

    return pl.pallas_call(
        run,
        out_shape=outs,
        in_specs=[inside] * len(args) + [ANY] * len(after),
        out_specs=list(outside) + [VMEM] * (len(outs) - len(outside)),
        scratch_shapes=scratch,
        compiler_params=PARAMS,
        cost_estimate=pl.CostEstimate(flops=flops, bytes_accessed=moved, transcendentals=0),
    )(*args, *after)


def copied(pairs, sems):
    copies = [pltpu.make_async_copy(source, target, sems.at[i]) for i, (source, target) in enumerate(pairs)]
    for copy in copies:
        copy.start()
    return copies


def cut_kernel(block, whole, last, near, far, sems):
    frames, rows = block.shape[:2]
    pairs = [
        (block.at[:, pl.ds(near_row(rows), 1)], near),
        (block.at[:, pl.ds(far_row(rows), 1)], far),
        (block.at[pl.ds(frames - 2, 2)], last),
        (block, whole),
    ]
    for copy in copied(pairs, sems):
        copy.wait()


def taps_kernel(kernel, taps, back_taps, held, sems):
    (copy,) = copied([(kernel, held)], sems)
    copy.wait()
    lay_taps(taps, held, False)
    lay_taps(back_taps, held, True)


def lay(pad, centre, time, near, far, corners, ahead):
    frames, rows = centre.shape[:2]
    place, above = near_row(rows + 2), far_row(rows + 2)
    own = pl.ds(0 if ahead else 2, frames)
    beyond = pl.ds(frames if ahead else 0, 2)
    pad[own, 1 : 1 + rows] = centre[...]
    pad[own, pl.ds(place, 1)] = near[...]
    pad[own, pl.ds(above, 1)] = far[...]
    pad[beyond, 1 : 1 + rows] = time[...]
    pad[beyond, pl.ds(place, 1)] = corners[:, 0:1]
    pad[beyond, pl.ds(above, 1)] = corners[:, 1:2]

    def clear(at):
        pad[at] = jnp.zeros_like(pad[at])

    line, tm = lax.axis_index("height"), lax.axis_index("tm")
    pl.when(line == 0)(lambda: clear((slice(None), slice(0, 1))))
    pl.when(line == lax.axis_size("height") - 1)(lambda: clear((slice(None), slice(rows + 1, rows + 2))))
    pl.when(tm == (lax.axis_size("tm") - 1 if ahead else 0))(lambda: clear((beyond,)))


def near_row(rows):
    return (1 - lax.axis_index("height") % 2) * (rows - 1)


def far_row(rows):
    return lax.axis_index("height") % 2 * (rows - 1)


def strips(block, last, near, far, ahead):
    frames, rows = block.shape[:2]
    last[...] = block[0:2] if ahead else block[frames - 2 :]
    near[...] = block[:, pl.ds(near_row(rows), 1)]
    far[...] = block[:, pl.ds(far_row(rows), 1)]


def down(value, columns):
    row = lax.broadcasted_iota(jnp.int32, value.shape, 0) % columns
    return jnp.where(row == 0, 0.0, pltpu.roll(value, 1, 0))


def up(value, columns):
    row = lax.broadcasted_iota(jnp.int32, value.shape, 0) % columns
    return jnp.where(row == columns - 1, 0.0, pltpu.roll(value, value.shape[0] - 1, 0))


def convolve(pad, taps, frame, row, rows, transposed):
    columns, channels = pad.shape[2:]
    parts = []
    for a, b in TAPS:
        t, h = (frame + 2 - a, row + 2 - b) if transposed else (frame + a, row + b)
        parts.append(pad[t, h : h + rows].reshape(rows * columns, channels))
    stacked = jnp.concatenate(parts, axis=1)
    product = jnp.dot(stacked, taps[...], preferred_element_type=jnp.float32)
    left, middle, right = (product[:, c * channels : (c + 1) * channels] for c in range(3))
    if transposed:
        left, right = right, left
    return down(left, columns) + middle + up(right, columns)


def lay_taps(taps, kernel, transposed):
    c_in, c_out = kernel.shape[3:]
    for place, (a, b) in enumerate(TAPS):
        for c in range(3):
            tap = kernel[a, b, c].T if transposed else kernel[a, b, c]
            taps[place * c_in : (place + 1) * c_in, c * c_out : (c + 1) * c_out] = tap


def blocks(frames, rows):
    return [(t, slice(h, h + 2)) for t in range(frames) for h in range(0, rows, 2)]


def first_kernel(centre, time, near, far, corners, taps, slope, hidden, last, near_out, far_out, pad):
    lay(pad, centre, time, near, far, corners, False)
    frames, rows = centre.shape[:2]
    for t, rows in blocks(frames, rows):
        z = convolve(pad, taps, t, rows.start, 2, False)
        s = jax.nn.sigmoid(z)
        slope[t, rows] = (s * (1.0 + z * (1.0 - s))).reshape(2, *slope.shape[2:])
        hidden[t, rows] = (z * s).astype(jnp.bfloat16).reshape(2, *hidden.shape[2:])
    strips(hidden, last, near_out, far_out, False)


def second_kernel(
    centre, time, near, far, corners, taps, cotangent, output, grad, last, near_out, far_out, pad
):
    lay(pad, centre, time, near, far, corners, False)
    frames, rows = centre.shape[:2]
    for t, rows in blocks(frames, rows):
        z = convolve(pad, taps, t, rows.start, 2, False)
        s = jax.nn.sigmoid(z)
        output[t, rows] = (z * s).astype(jnp.bfloat16).reshape(2, *output.shape[2:])
        steep = (s * (1.0 + z * (1.0 - s))).reshape(2, *grad.shape[2:])
        grad[t, rows] = (cotangent[t, rows].astype(jnp.float32) * steep).astype(jnp.bfloat16)
    strips(grad, last, near_out, far_out, True)


def back_kernel(centre, time, near, far, corners, taps, made, output, grad, ended, pad, sems):
    copy = pltpu.make_async_copy(made, output, sems.at[0])
    copy.start()
    lay(pad, centre, time, near, far, corners, True)
    frames, rows = centre.shape[:2]
    for t, rows in blocks(frames, rows):
        z = convolve(pad, taps, t, rows.start, 2, True)
        grad[t, rows] = z.astype(jnp.bfloat16).reshape(2, *grad.shape[2:])
    ended[...] = jnp.zeros_like(ended)
    copy.wait()


def back_slope_kernel(
    centre, time, near, far, corners, taps, slope, grad, last, near_out, far_out, pad
):
    lay(pad, centre, time, near, far, corners, True)
    frames, rows = centre.shape[:2]
    for t, rows in blocks(frames, rows):
        z = convolve(pad, taps, t, rows.start, 2, True).reshape(2, *grad.shape[2:])
        grad[t, rows] = (z * slope[t, rows]).astype(jnp.bfloat16)
    strips(grad, last, near_out, far_out, True)


def weight_kernel(centre, time, near, far, corners, grad, keep, send, pad, moved):
    lay(pad, centre, time, near, far, corners, False)
    frames, rows, columns, channels = centre.shape
    cells = frames * rows * columns
    core = lax.axis_index("tm") % 2
    wide = grad[...].reshape(cells, channels).astype(jnp.float32)
    moved[:, :channels] = up(wide, columns).astype(jnp.bfloat16)
    moved[:, channels : 2 * channels] = grad[...].reshape(cells, channels)
    moved[:, 2 * channels :] = down(wide, columns).astype(jnp.bfloat16)
    dims = (((0,), (0,)), ((), ()))
    half = channels // 2
    for place, (a, b) in enumerate(TAPS):
        block = pad[a : a + frames, b : b + rows].reshape(cells, channels)
        product = lax.dot_general(block, moved[...], dims, preferred_element_type=jnp.float32)
        for c in range(3):
            part = product[:, c * channels : (c + 1) * channels]
            mine = jnp.where(core == 0, part[:half], part[half:])
            other = jnp.where(core == 0, part[half:], part[:half])
            keep[:, 3 * place + c] = mine.reshape(4, -1, channels)
            send[:, 3 * place + c] = other.astype(jnp.bfloat16).reshape(4, -1, channels)
    for out in (keep, send):
        out[:, 27:] = jnp.zeros_like(out[:, 27:])


def scatter_kernel(keep_one, came_one, keep_two, came_two, mine, *parts):
    x = lax.axis_index("height") % 4
    over_one, over_three, plain_one, plain_three, later_one, later_three = parts
    targets = ((mine.at[0], plain_one, over_one, later_three), (mine.at[1], later_one, over_three, plain_three))
    for (keep, came), outs in zip(((keep_one, came_one), (keep_two, came_two)), targets, strict=True):
        for d in (2, 1, 3, 0):
            total = keep[x ^ d] + came[x ^ d].astype(jnp.float32)
            outs[d][...] = total.reshape(outs[d].shape).astype(outs[d].dtype)


def relay_kernel(later_one, later_three, came_one, came_three, to_one, to_three):
    to_one[...] = (later_one[...] + came_three[...].astype(jnp.float32)).astype(jnp.bfloat16)
    to_three[...] = (later_three[...] + came_one[...].astype(jnp.float32)).astype(jnp.bfloat16)


def second_scatter_kernel(own, one_first, three_first, one_second, three_second, mine, *sent):
    y = lax.axis_index("height") // 4
    for d, out in enumerate((mine, *sent)):
        for k, (one, three) in enumerate(((one_first, three_first), (one_second, three_second))):
            came = one[y ^ d].astype(jnp.float32) + three[y ^ d].astype(jnp.float32)
            out[k] = (own[k, y ^ d] + came).astype(out.dtype)


def add_kernel(own, one, two, three, out):
    own, one, two, three = (ref[...].astype(jnp.float32) for ref in (own, one, two, three))
    out[...] = ((own + one) + (two + three)).astype(out.dtype)


def join_kernel(own, one, three, two, out):
    y = lax.axis_index("height") // 4
    for d, part in enumerate((own, one, two, three)):
        out[:, y ^ d] = part[...]


def gather_kernel(scale, *refs):
    pieces, made, outs, clip_grad, (held, sems) = refs[:8], refs[8], refs[9:11], refs[11], refs[12:]
    x, core = lax.axis_index("height") % 4, lax.axis_index("tm") % 2
    taps = outs[0].shape[0]
    copies = [pltpu.make_async_copy(made, clip_grad, sems.at[8])]
    copies[0].start()
    for k, out in enumerate(outs):
        for q in range(4):
            first, count = 7 * q, min(7, taps - 7 * q)
            for place, d in enumerate((0, 1, 3, 2)):
                for half in range(2):
                    block = pieces[4 * half + place][k, q, :count].astype(jnp.float32) * scale
                    held[k, pl.ds(first, count), pl.ds((core ^ half) * 4 + (x ^ d), 1)] = block[:, None]
            part = pl.ds(first, count)
            copies.append(pltpu.make_async_copy(held.at[k, part], out.at[part], sems.at[4 * k + q]))
            copies[-1].start()
    for copy in copies:
        copy.wait()


def swap(value, mask):
    return lax.ppermute(value, ALL, [(i, i ^ mask) for i in range(lax.axis_size(ALL))])


def started(one, two):
    _, taps, part, channels = one[0].shape
    shape = (4, taps // 4, part, channels)
    f32 = jax.ShapeDtypeStruct((2, *shape), jnp.float32)
    bf16 = jax.ShapeDtypeStruct(shape, jnp.bfloat16)
    halves = (one[0], swap(one[1], 16), two[0], swap(two[1], 16))
    later = jax.ShapeDtypeStruct(shape, jnp.float32)
    return call(scatter_kernel, [f32, *4 * [bf16], later, later], [], 16 * math.prod(shape), *halves)


def summed(quarters, scale, cornered, ended, made):
    mine, over_one, over_three, plain_one, plain_three, *later = quarters
    shape = mine.shape
    part, channels = shape[3:]
    size = math.prod(shape)
    whole = jax.ShapeDtypeStruct(shape, jnp.bfloat16)
    half = jax.ShapeDtypeStruct(shape[1:], jnp.bfloat16)
    came = swap(over_one, 1), swap(over_three, 3)
    one_first, three_second = swap(plain_one, 1), swap(plain_three, 3)
    to_one, to_three = call(relay_kernel, [half, half], [], size, *later, *came)
    one_second, three_first = swap(to_one, 1), swap(to_three, 3)
    came = one_first, three_first, one_second, three_second
    quarter = (shape[0], *shape[2:])
    small = jax.ShapeDtypeStruct(quarter, jnp.bfloat16)
    exact = jax.ShapeDtypeStruct(quarter, jnp.float32)
    mine, *sent = call(
        second_scatter_kernel, [exact, small, small, small], [], 4 * size, mine, *came
    )
    one, two, three = (swap(value, 4 * d) for d, value in enumerate(sent, 1))
    (total,) = call(add_kernel, [small], [], size, mine, two, one, three, after=cornered)
    one, two, three = (swap(total, mask) for mask in (64, 32, 96))
    (total,) = call(add_kernel, [small], [], size, total, one, three, two, after=ended)
    one, two, three = (swap(total, 4 * d) for d in (1, 2, 3))
    (total,) = call(join_kernel, [whole], [], size, total, one, three, two)
    pieces = [total] + [swap(total, d) for d in (1, 3, 2)]
    pieces += [swap(value, 16) for value in pieces]
    out_shape = (27, 8, part, channels)
    outs = call(
        functools.partial(gather_kernel, scale),
        [jax.ShapeDtypeStruct(out_shape, jnp.float32)] * 2 + [jax.ShapeDtypeStruct(made.shape, made.dtype)],
        [pltpu.VMEM((2, *out_shape), jnp.float32), pltpu.SemaphoreType.DMA((9,))],
        8 * size,
        *pieces,
        made,
        outside=(HBM, HBM, HBM),
    )
    return [out.reshape(3, 3, 3, channels, channels) for out in outs[:2]] + list(outs[2:])


def time_route(ahead):
    count = lax.axis_size("tm")
    step = -1 if ahead else 1
    return [(i, (i + step) % count) for i in range(count)]


def pack_kernel(near, far, out, *, first):
    out[:, 0:1] = near[first : first + 2]
    out[:, 1:2] = far[first : first + 2]


def exchanged(last, near, far, ahead):
    line = lax.axis_size("height")
    time = lax.ppermute(last, "tm", time_route(ahead))
    near = lax.ppermute(near, "height", [(i, i ^ 1) for i in range(line)])
    far = lax.ppermute(far, "height", [(i, (i - 1 if i % 2 == 0 else i + 1) % line) for i in range(line)])
    return time, near, far


def cornered(time, near, far, ahead, after=()):
    shape = jax.ShapeDtypeStruct((2, 2, *near.shape[2:]), near.dtype)
    kernel = functools.partial(pack_kernel, first=0 if ahead else near.shape[0] - 2)
    if after:
        (rows,) = call(kernel, [shape], [], 0, near, far, after=after)
    else:
        rows = jnp.concatenate([near, far], axis=1)
        rows = rows[:2] if ahead else rows[-2:]
    return time, near, far, lax.ppermute(rows, "tm", time_route(ahead))


def body(clip, first_weight, second_weight, cotangent):
    _, frames, rows, columns, channels = clip.shape
    cells = frames * rows * columns
    clip, cotangent = clip[0], cotangent[0]
    flops = 2 * cells * 27 * channels * channels
    shape = (frames, rows, columns, channels)
    bf16 = jax.ShapeDtypeStruct(shape, jnp.bfloat16)
    f32 = jax.ShapeDtypeStruct(shape, jnp.float32)
    last = jax.ShapeDtypeStruct((2, *shape[1:]), jnp.bfloat16)
    line = jax.ShapeDtypeStruct((frames, 1, *shape[2:]), jnp.bfloat16)
    quarters = (4, 28, channels // 8, channels)
    keep = jax.ShapeDtypeStruct(quarters, jnp.float32)
    send = jax.ShapeDtypeStruct(quarters, jnp.bfloat16)
    pad = pltpu.VMEM((frames + 2, rows + 2, columns, channels), jnp.bfloat16)
    taps = pltpu.VMEM((9 * channels, 3 * channels), jnp.bfloat16)
    back_taps = pltpu.VMEM((3 * channels, 9 * channels), jnp.bfloat16)
    moved = pltpu.VMEM((cells, 3 * channels), jnp.bfloat16)
    scale = 1.0 / math.sqrt(cells * lax.axis_size(ALL))

    whole, *cut = call(
        cut_kernel, [bf16, last, line, line], [pltpu.SemaphoreType.DMA((4,))], 0, clip, inside=HBM
    )
    clip_edges = cornered(*exchanged(*cut, False), False)
    layout = jax.ShapeDtypeStruct(taps.shape, taps.dtype)
    held = [pltpu.VMEM(first_weight.shape, first_weight.dtype), pltpu.SemaphoreType.DMA((1,))]
    first_taps, first_back = call(taps_kernel, [layout, layout], held, 0, first_weight, inside=HBM)
    slope, hidden, *cut = call(
        first_kernel, [f32, bf16, last, line, line], [pad], flops, whole, *clip_edges, first_taps
    )
    hidden_edges = cornered(*exchanged(*cut, False), False)
    second_taps, second_back = call(taps_kernel, [layout, layout], held, 0, second_weight, after=cut[1:2], inside=HBM)
    made, grad_two, *cut = call(
        second_kernel,
        [bf16, bf16, last, line, line],
        [pad],
        flops,
        hidden,
        *hidden_edges,
        second_taps,
        cotangent,
    )
    two_edges = cornered(*exchanged(*cut, True), True)
    second_terms = call(weight_kernel, [keep, send], [pad, moved], flops, hidden, *hidden_edges, grad_two)
    grad_one, *cut = call(
        back_slope_kernel,
        [bf16, last, line, line],
        [pad],
        flops,
        grad_two,
        *two_edges,
        second_back,
        slope,
    )
    one_edges = exchanged(*cut, True)
    first_terms = call(weight_kernel, [keep, send], [pad, moved], flops, whole, *clip_edges, grad_one)
    quarters = started(first_terms, second_terms)
    one_edges = cornered(*one_edges, True, after=quarters[:1])
    ended = jax.ShapeDtypeStruct((8, 128), jnp.float32)
    output, grad, ended = call(
        back_kernel,
        [bf16, bf16, ended],
        [pad, pltpu.SemaphoreType.DMA((1,))],
        flops,
        grad_one,
        *one_edges,
        first_back,
        made,
        outside=(HBM,),
    )
    first_grad, second_grad, clip_grad = summed(quarters, scale, one_edges[3:], (ended,), grad)
    return output[None], clip_grad[None], first_grad, second_grad


def solution(mesh):
    block = P("dp", "tm", "height", None, None)
    return jax.shard_map(
        body,
        mesh=mesh,
        in_specs=(block, P(), P(), block),
        out_specs=(block, block, P(), P()),
        check_vma=False,
    )
```

```python
import functools
import math

import jax
import jax.numpy as jnp
from jax import lax
from jax.experimental import pallas as pl
from jax.experimental.pallas import tpu as pltpu
from jax.sharding import PartitionSpec as P

ALL = ("dp", "tm", "height")
PARAMS = pltpu.CompilerParams(vmem_limit_bytes=48 * 1024 * 1024)
VMEM = pl.BlockSpec(memory_space=pltpu.VMEM)
HBM = pl.BlockSpec(memory_space=pltpu.HBM)
ANY = pl.BlockSpec(memory_space=pl.ANY)
TAPS = [(a, b) for a in range(3) for b in range(3)]


def call(kernel, outs, scratch, flops, *args, after=(), inside=VMEM, outside=()):
    moved = sum(x.size * x.dtype.itemsize for x in (*args, *outs))

    def run(*refs):
        kernel(*refs[: len(args)], *refs[len(args) + len(after) :])

    return pl.pallas_call(
        run,
        out_shape=outs,
        in_specs=[inside] * len(args) + [ANY] * len(after),
        out_specs=list(outside) + [VMEM] * (len(outs) - len(outside)),
        scratch_shapes=scratch,
        compiler_params=PARAMS,
        cost_estimate=pl.CostEstimate(flops=flops, bytes_accessed=moved, transcendentals=0),
    )(*args, *after)


def copied(pairs, sems):
    copies = [pltpu.make_async_copy(source, target, sems.at[i]) for i, (source, target) in enumerate(pairs)]
    for copy in copies:
        copy.start()
    return copies


def cut_kernel(block, whole, last, near, far, sems):
    frames, rows = block.shape[:2]
    pairs = [
        (block.at[:, pl.ds(near_row(rows), 1)], near),
        (block.at[:, pl.ds(far_row(rows), 1)], far),
        (block.at[pl.ds(frames - 2, 2)], last),
        (block, whole),
    ]
    for copy in copied(pairs, sems):
        copy.wait()


def taps_kernel(kernel, taps, back_taps, held, sems):
    (copy,) = copied([(kernel, held)], sems)
    copy.wait()
    lay_taps(taps, held, False)
    lay_taps(back_taps, held, True)


def lay(pad, centre, time, near, far, corners, ahead):
    frames, rows = centre.shape[:2]
    place, above = near_row(rows + 2), far_row(rows + 2)
    own = pl.ds(0 if ahead else 2, frames)
    beyond = pl.ds(frames if ahead else 0, 2)
    pad[own, 1 : 1 + rows] = centre[...]
    pad[own, pl.ds(place, 1)] = near[...]
    pad[own, pl.ds(above, 1)] = far[...]
    pad[beyond, 1 : 1 + rows] = time[...]
    pad[beyond, pl.ds(place, 1)] = corners[:, 0:1]
    pad[beyond, pl.ds(above, 1)] = corners[:, 1:2]

    def clear(at):
        pad[at] = jnp.zeros_like(pad[at])

    line, tm = lax.axis_index("height"), lax.axis_index("tm")
    pl.when(line == 0)(lambda: clear((slice(None), slice(0, 1))))
    pl.when(line == lax.axis_size("height") - 1)(lambda: clear((slice(None), slice(rows + 1, rows + 2))))
    pl.when(tm == (lax.axis_size("tm") - 1 if ahead else 0))(lambda: clear((beyond,)))


def near_row(rows):
    return (1 - lax.axis_index("height") % 2) * (rows - 1)


def far_row(rows):
    return lax.axis_index("height") % 2 * (rows - 1)


def strips(block, last, near, far, ahead):
    frames, rows = block.shape[:2]
    last[...] = block[0:2] if ahead else block[frames - 2 :]
    near[...] = block[:, pl.ds(near_row(rows), 1)]
    far[...] = block[:, pl.ds(far_row(rows), 1)]


def down(value, columns):
    row = lax.broadcasted_iota(jnp.int32, value.shape, 0) % columns
    return jnp.where(row == 0, 0.0, pltpu.roll(value, 1, 0))


def up(value, columns):
    row = lax.broadcasted_iota(jnp.int32, value.shape, 0) % columns
    return jnp.where(row == columns - 1, 0.0, pltpu.roll(value, value.shape[0] - 1, 0))


def convolve(pad, taps, frame, row, rows, transposed):
    columns, channels = pad.shape[2:]
    parts = []
    for a, b in TAPS:
        t, h = (frame + 2 - a, row + 2 - b) if transposed else (frame + a, row + b)
        parts.append(pad[t, h : h + rows].reshape(rows * columns, channels))
    stacked = jnp.concatenate(parts, axis=1)
    product = jnp.dot(stacked, taps[...], preferred_element_type=jnp.float32)
    left, middle, right = (product[:, c * channels : (c + 1) * channels] for c in range(3))
    if transposed:
        left, right = right, left
    return down(left, columns) + middle + up(right, columns)


def lay_taps(taps, kernel, transposed):
    c_in, c_out = kernel.shape[3:]
    for place, (a, b) in enumerate(TAPS):
        for c in range(3):
            tap = kernel[a, b, c].T if transposed else kernel[a, b, c]
            taps[place * c_in : (place + 1) * c_in, c * c_out : (c + 1) * c_out] = tap


def blocks(frames, rows):
    return [(t, slice(h, h + 1)) for t in range(frames) for h in range(rows)]


def first_kernel(centre, time, near, far, corners, taps, slope, hidden, last, near_out, far_out, pad):
    lay(pad, centre, time, near, far, corners, False)
    frames, rows = centre.shape[:2]
    for t, rows in blocks(frames, rows):
        z = convolve(pad, taps, t, rows.start, 1, False)
        s = jax.nn.sigmoid(z)
        slope[t, rows] = (s * (1.0 + z * (1.0 - s))).reshape(1, *slope.shape[2:])
        hidden[t, rows] = (z * s).astype(jnp.bfloat16).reshape(1, *hidden.shape[2:])
    strips(hidden, last, near_out, far_out, False)


def second_kernel(
    centre, time, near, far, corners, taps, cotangent, output, grad, last, near_out, far_out, pad
):
    lay(pad, centre, time, near, far, corners, False)
    frames, rows = centre.shape[:2]
    for t, rows in blocks(frames, rows):
        z = convolve(pad, taps, t, rows.start, 1, False)
        s = jax.nn.sigmoid(z)
        output[t, rows] = (z * s).astype(jnp.bfloat16).reshape(1, *output.shape[2:])
        steep = (s * (1.0 + z * (1.0 - s))).reshape(1, *grad.shape[2:])
        grad[t, rows] = (cotangent[t, rows].astype(jnp.float32) * steep).astype(jnp.bfloat16)
    strips(grad, last, near_out, far_out, True)


def back_kernel(centre, time, near, far, corners, taps, made, output, grad, ended, pad, sems):
    copy = pltpu.make_async_copy(made, output, sems.at[0])
    copy.start()
    lay(pad, centre, time, near, far, corners, True)
    frames, rows = centre.shape[:2]
    for t, rows in blocks(frames, rows):
        z = convolve(pad, taps, t, rows.start, 1, True)
        grad[t, rows] = z.astype(jnp.bfloat16).reshape(1, *grad.shape[2:])
    ended[...] = jnp.zeros_like(ended)
    copy.wait()


def back_slope_kernel(
    centre, time, near, far, corners, taps, slope, grad, last, near_out, far_out, pad
):
    lay(pad, centre, time, near, far, corners, True)
    frames, rows = centre.shape[:2]
    for t, rows in blocks(frames, rows):
        z = convolve(pad, taps, t, rows.start, 1, True).reshape(1, *grad.shape[2:])
        grad[t, rows] = (z * slope[t, rows]).astype(jnp.bfloat16)
    strips(grad, last, near_out, far_out, True)


def weight_kernel(centre, time, near, far, corners, grad, keep, send, pad, moved):
    lay(pad, centre, time, near, far, corners, False)
    frames, rows, columns, channels = centre.shape
    cells = frames * rows * columns
    core = lax.axis_index("tm") % 2
    wide = grad[...].reshape(cells, channels).astype(jnp.float32)
    moved[:, :channels] = up(wide, columns).astype(jnp.bfloat16)
    moved[:, channels : 2 * channels] = grad[...].reshape(cells, channels)
    moved[:, 2 * channels :] = down(wide, columns).astype(jnp.bfloat16)
    dims = (((0,), (0,)), ((), ()))
    half = channels // 2
    for place, (a, b) in enumerate(TAPS):
        block = pad[a : a + frames, b : b + rows].reshape(cells, channels)
        product = lax.dot_general(block, moved[...], dims, preferred_element_type=jnp.float32)
        for c in range(3):
            part = product[:, c * channels : (c + 1) * channels]
            mine = jnp.where(core == 0, part[:half], part[half:])
            other = jnp.where(core == 0, part[half:], part[:half])
            keep[:, 3 * place + c] = mine.reshape(4, -1, channels)
            send[:, 3 * place + c] = other.astype(jnp.bfloat16).reshape(4, -1, channels)
    for out in (keep, send):
        out[:, 27:] = jnp.zeros_like(out[:, 27:])


def scatter_kernel(keep_one, came_one, keep_two, came_two, mine, *parts):
    x = lax.axis_index("height") % 4
    over_one, over_three, plain_one, plain_three, later_one, later_three = parts
    targets = ((mine.at[0], plain_one, over_one, later_three), (mine.at[1], later_one, over_three, plain_three))
    for (keep, came), outs in zip(((keep_one, came_one), (keep_two, came_two)), targets, strict=True):
        for d in (2, 1, 3, 0):
            total = keep[x ^ d] + came[x ^ d].astype(jnp.float32)
            outs[d][...] = total.reshape(outs[d].shape).astype(outs[d].dtype)


def relay_kernel(later_one, later_three, came_one, came_three, to_one, to_three):
    to_one[...] = (later_one[...] + came_three[...].astype(jnp.float32)).astype(jnp.bfloat16)
    to_three[...] = (later_three[...] + came_one[...].astype(jnp.float32)).astype(jnp.bfloat16)


def second_scatter_kernel(own, one_first, three_first, one_second, three_second, mine, *sent):
    y = lax.axis_index("height") // 4
    for d, out in enumerate((mine, *sent)):
        for k, (one, three) in enumerate(((one_first, three_first), (one_second, three_second))):
            came = one[y ^ d].astype(jnp.float32) + three[y ^ d].astype(jnp.float32)
            out[k] = (own[k, y ^ d] + came).astype(out.dtype)


def add_kernel(own, one, two, three, out):
    own, one, two, three = (ref[...].astype(jnp.float32) for ref in (own, one, two, three))
    out[...] = ((own + one) + (two + three)).astype(out.dtype)


def join_kernel(own, one, three, two, out):
    y = lax.axis_index("height") // 4
    for d, part in enumerate((own, one, two, three)):
        out[:, y ^ d] = part[...]


def gather_kernel(scale, *refs):
    pieces, made, outs, clip_grad, (held, sems) = refs[:8], refs[8], refs[9:11], refs[11], refs[12:]
    x, core = lax.axis_index("height") % 4, lax.axis_index("tm") % 2
    taps = outs[0].shape[0]
    copies = [pltpu.make_async_copy(made, clip_grad, sems.at[8])]
    copies[0].start()
    for k, out in enumerate(outs):
        for q in range(4):
            first, count = 7 * q, min(7, taps - 7 * q)
            for place, d in enumerate((0, 1, 3, 2)):
                for half in range(2):
                    block = pieces[4 * half + place][k, q, :count].astype(jnp.float32) * scale
                    held[k, pl.ds(first, count), pl.ds((core ^ half) * 4 + (x ^ d), 1)] = block[:, None]
            part = pl.ds(first, count)
            copies.append(pltpu.make_async_copy(held.at[k, part], out.at[part], sems.at[4 * k + q]))
            copies[-1].start()
    for copy in copies:
        copy.wait()


def swap(value, mask):
    return lax.ppermute(value, ALL, [(i, i ^ mask) for i in range(lax.axis_size(ALL))])


def started(one, two):
    _, taps, part, channels = one[0].shape
    shape = (4, taps // 4, part, channels)
    f32 = jax.ShapeDtypeStruct((2, *shape), jnp.float32)
    bf16 = jax.ShapeDtypeStruct(shape, jnp.bfloat16)
    halves = (one[0], swap(one[1], 16), two[0], swap(two[1], 16))
    later = jax.ShapeDtypeStruct(shape, jnp.float32)
    return call(scatter_kernel, [f32, *4 * [bf16], later, later], [], 16 * math.prod(shape), *halves)


def summed(quarters, scale, cornered, ended, made):
    mine, over_one, over_three, plain_one, plain_three, *later = quarters
    shape = mine.shape
    part, channels = shape[3:]
    size = math.prod(shape)
    whole = jax.ShapeDtypeStruct(shape, jnp.bfloat16)
    half = jax.ShapeDtypeStruct(shape[1:], jnp.bfloat16)
    came = swap(over_one, 1), swap(over_three, 3)
    one_first, three_second = swap(plain_one, 1), swap(plain_three, 3)
    to_one, to_three = call(relay_kernel, [half, half], [], size, *later, *came)
    one_second, three_first = swap(to_one, 1), swap(to_three, 3)
    came = one_first, three_first, one_second, three_second
    quarter = (shape[0], *shape[2:])
    small = jax.ShapeDtypeStruct(quarter, jnp.bfloat16)
    exact = jax.ShapeDtypeStruct(quarter, jnp.float32)
    mine, *sent = call(
        second_scatter_kernel, [exact, small, small, small], [], 4 * size, mine, *came
    )
    one, two, three = (swap(value, 4 * d) for d, value in enumerate(sent, 1))
    (total,) = call(add_kernel, [small], [], size, mine, two, one, three, after=cornered)
    one, two, three = (swap(total, mask) for mask in (64, 32, 96))
    (total,) = call(add_kernel, [small], [], size, total, one, three, two, after=ended)
    one, two, three = (swap(total, 4 * d) for d in (1, 2, 3))
    (total,) = call(join_kernel, [whole], [], size, total, one, three, two)
    pieces = [total] + [swap(total, d) for d in (1, 3, 2)]
    pieces += [swap(value, 16) for value in pieces]
    out_shape = (27, 8, part, channels)
    outs = call(
        functools.partial(gather_kernel, scale),
        [jax.ShapeDtypeStruct(out_shape, jnp.float32)] * 2 + [jax.ShapeDtypeStruct(made.shape, made.dtype)],
        [pltpu.VMEM((2, *out_shape), jnp.float32), pltpu.SemaphoreType.DMA((9,))],
        8 * size,
        *pieces,
        made,
        outside=(HBM, HBM, HBM),
    )
    return [out.reshape(3, 3, 3, channels, channels) for out in outs[:2]] + list(outs[2:])


def time_route(ahead):
    count = lax.axis_size("tm")
    step = -1 if ahead else 1
    return [(i, (i + step) % count) for i in range(count)]


def pack_kernel(near, far, out, *, first):
    out[:, 0:1] = near[first : first + 2]
    out[:, 1:2] = far[first : first + 2]


def exchanged(last, near, far, ahead):
    line = lax.axis_size("height")
    time = lax.ppermute(last, "tm", time_route(ahead))
    near = lax.ppermute(near, "height", [(i, i ^ 1) for i in range(line)])
    far = lax.ppermute(far, "height", [(i, (i - 1 if i % 2 == 0 else i + 1) % line) for i in range(line)])
    return time, near, far


def cornered(time, near, far, ahead, after=()):
    shape = jax.ShapeDtypeStruct((2, 2, *near.shape[2:]), near.dtype)
    kernel = functools.partial(pack_kernel, first=0 if ahead else near.shape[0] - 2)
    if after:
        (rows,) = call(kernel, [shape], [], 0, near, far, after=after)
    else:
        rows = jnp.concatenate([near, far], axis=1)
        rows = rows[:2] if ahead else rows[-2:]
    return time, near, far, lax.ppermute(rows, "tm", time_route(ahead))


def body(clip, first_weight, second_weight, cotangent):
    _, frames, rows, columns, channels = clip.shape
    cells = frames * rows * columns
    clip, cotangent = clip[0], cotangent[0]
    flops = 2 * cells * 27 * channels * channels
    shape = (frames, rows, columns, channels)
    bf16 = jax.ShapeDtypeStruct(shape, jnp.bfloat16)
    f32 = jax.ShapeDtypeStruct(shape, jnp.float32)
    last = jax.ShapeDtypeStruct((2, *shape[1:]), jnp.bfloat16)
    line = jax.ShapeDtypeStruct((frames, 1, *shape[2:]), jnp.bfloat16)
    quarters = (4, 28, channels // 8, channels)
    keep = jax.ShapeDtypeStruct(quarters, jnp.float32)
    send = jax.ShapeDtypeStruct(quarters, jnp.bfloat16)
    pad = pltpu.VMEM((frames + 2, rows + 2, columns, channels), jnp.bfloat16)
    taps = pltpu.VMEM((9 * channels, 3 * channels), jnp.bfloat16)
    back_taps = pltpu.VMEM((3 * channels, 9 * channels), jnp.bfloat16)
    moved = pltpu.VMEM((cells, 3 * channels), jnp.bfloat16)
    scale = 1.0 / math.sqrt(cells * lax.axis_size(ALL))

    whole, *cut = call(
        cut_kernel, [bf16, last, line, line], [pltpu.SemaphoreType.DMA((4,))], 0, clip, inside=HBM
    )
    clip_edges = cornered(*exchanged(*cut, False), False)
    layout = jax.ShapeDtypeStruct(taps.shape, taps.dtype)
    held = [pltpu.VMEM(first_weight.shape, first_weight.dtype), pltpu.SemaphoreType.DMA((1,))]
    first_taps, first_back = call(taps_kernel, [layout, layout], held, 0, first_weight, inside=HBM)
    slope, hidden, *cut = call(
        first_kernel, [f32, bf16, last, line, line], [pad], flops, whole, *clip_edges, first_taps
    )
    hidden_edges = cornered(*exchanged(*cut, False), False)
    second_taps, second_back = call(taps_kernel, [layout, layout], held, 0, second_weight, after=cut[1:2], inside=HBM)
    made, grad_two, *cut = call(
        second_kernel,
        [bf16, bf16, last, line, line],
        [pad],
        flops,
        hidden,
        *hidden_edges,
        second_taps,
        cotangent,
    )
    two_edges = cornered(*exchanged(*cut, True), True)
    second_terms = call(weight_kernel, [keep, send], [pad, moved], flops, hidden, *hidden_edges, grad_two)
    grad_one, *cut = call(
        back_slope_kernel,
        [bf16, last, line, line],
        [pad],
        flops,
        grad_two,
        *two_edges,
        second_back,
        slope,
    )
    one_edges = exchanged(*cut, True)
    first_terms = call(weight_kernel, [keep, send], [pad, moved], flops, whole, *clip_edges, grad_one)
    quarters = started(first_terms, second_terms)
    one_edges = cornered(*one_edges, True, after=quarters[:1])
    ended = jax.ShapeDtypeStruct((8, 128), jnp.float32)
    output, grad, ended = call(
        back_kernel,
        [bf16, bf16, ended],
        [pad, pltpu.SemaphoreType.DMA((1,))],
        flops,
        grad_one,
        *one_edges,
        first_back,
        made,
        outside=(HBM,),
    )
    first_grad, second_grad, clip_grad = summed(quarters, scale, one_edges[3:], (ended,), grad)
    return output[None], clip_grad[None], first_grad, second_grad


def solution(mesh):
    block = P("dp", "tm", "height", None, None)
    return jax.shard_map(
        body,
        mesh=mesh,
        in_specs=(block, P(), P(), block),
        out_specs=(block, block, P(), P()),
        check_vma=False,
    )
```
